32 devices in a mesh: parts: 2 (over y), expert: 4 (over z), replica: 4 (over x, core).
Axes of the slice: x: 2, y: 2, z: 4, core: 2. Of those that a mesh axis runs over, the one named last changes fastest.
Arguments:
- tokens: bfloat16 [4096, 2048], P(('parts', 'expert', 'replica')), parts along dimension 0, may hold values from -6 to 6
- out_grad: bfloat16 [4096, 2048], P(('parts', 'expert', 'replica')), parts along dimension 0, may hold values from -4 to 4
- expert_ids: int32 [4096, 2], P(('parts', 'expert', 'replica')), parts along dimension 0, may hold values from 0 to 3, all different within a row; in each aligned block of 128 rows (0 to 127, 128 to 255, ...) at most 128 rows name the same one
- gates: bfloat16 [4096, 2], P(('parts', 'expert', 'replica')), parts along dimension 0, may hold values from 0.099609375 to 1
- gate_weight: bfloat16 [4, 2048, 1024], P('expert', None, 'replica'), may hold values from -0.125 to 0.125
- up_weight: bfloat16 [4, 2048, 1024], P('expert', None, 'replica'), may hold values from -0.125 to 0.125
- down_weight: bfloat16 [4, 2048, 1024], P('expert', None, 'replica'), may hold values from -0.125 to 0.125
Outputs:
- token_grad: bfloat16 [4096, 2048], P(('parts', 'expert', 'replica')), parts along dimension 0
- gate_grad: bfloat16 [4096, 2], P(('parts', 'expert', 'replica')), parts along dimension 0
- gate_weight_grad: bfloat16 [8, 2048, 1024], P(('parts', 'expert'), None, 'replica'), parts along dimension 0
- up_weight_grad: bfloat16 [8, 2048, 1024], P(('parts', 'expert'), None, 'replica'), parts along dimension 0
- down_weight_grad: bfloat16 [8, 2048, 1024], P(('parts', 'expert'), None, 'replica'), parts along dimension 0
The draws below stay inside these ranges and needn't reach their ends.
There are 2 independent parts, one for each index of `parts`. The reference program is written for one: setup_inputs(seed, part) draws one part's arguments, and reference() takes and returns one part's arrays. A program takes and returns all parts, laid end to end along the dimension named above; an argument that names none is the same for every part. Nothing has to cross between parts.
Inputs may be any that keep to these rules, and one draw needn't show every extreme that they name: `expert_ids`: among the 128 rows of one device (aligned blocks), no expert is named by more than 128 rows, and in some blocks one expert is named by exactly 128 rows; each row names two different experts; busy experts carry several times the mean load.
All inputs are finite; a program needn't handle non-finite values.
Results may differ from the reference program's by a relative error of at most 0.009.
Values may be sent and summed in bfloat16 or wider, within the bound.
No kernel may reach another device: no remote copies, remote signals or barrier semaphores. Data moves between devices by JAX's collectives and lax.ppermute only.
A program may use at most 128 MiB of HBM per device.

```python
import math
import jax
import jax.numpy as jnp
import numpy as np
from jax import lax

D = 2048
H = 1024
TOK_DEV = 128
EXPERTS = 4
MOST = 128
TOKENS = 2048
N_EXPERT = 4
N_REPLICA = 4


def levels(key, shape, shards, least, largest):
    gain, own = 1.0, jax.random.fold_in(key, 6)
    for position, blocks in shards:
        draws = jnp.exp(jax.random.uniform(jax.random.fold_in(own, position), (blocks,), jnp.float32, least / len(shards), largest / len(shards)))
        gain = gain * jnp.repeat(draws, shape[position] // blocks).reshape([-1 if axis == position else 1 for axis in range(len(shape))])
    return gain


def assign_block(rng, own, number, rows, number_of, top, reach, lean):
    sequence = jax.random.permutation(rng, number_of)
    heavy_load, common = load_shares(number_of, rows * top, reach, lean, True), load_shares(number_of, rows * top, reach, lean, False)
    places = jnp.arange(number_of)

    def named(lengths, turn):
        used = int((lengths > 0).sum())
        fixed = max(1, used // 4)
        shifted = fixed + (places - fixed + turn * (used - fixed)) % max(1, number_of - fixed)
        return jnp.zeros((number_of,), jnp.int32).at[sequence[jnp.where(places < fixed, places, shifted)]].set(jnp.asarray(lengths, jnp.int32))

    lengths = jnp.where(number % 4 == 0, named(heavy_load, number // 4), named(common, number - number // 4 - 1))
    mixed = jax.random.permutation(jax.random.fold_in(own, 3), number_of)
    donor, receiver = mixed[0:number_of // 2 * 2:2], mixed[1:number_of // 2 * 2:2]
    room = jnp.minimum(lengths[donor] - 1, reach - lengths[receiver]) // 2
    room = jnp.where((donor == sequence[0]) | (receiver == sequence[0]) | (lengths[receiver] == 0), 0, jnp.maximum(room, 0))
    shifted = jax.random.randint(jax.random.fold_in(own, 4), (number_of // 2,), 0, 1 << 20) % (room + 1)
    lengths = lengths.at[donor].add(-shifted).at[receiver].add(shifted)
    labels = jnp.searchsorted(jnp.cumsum(lengths), jnp.arange(rows * top), side="right").astype(jnp.int32)
    listing = labels.reshape(top, rows).T
    listing = listing[jax.random.permutation(jax.random.fold_in(own, 1), rows)]
    turn = jax.random.randint(jax.random.fold_in(own, 2), (rows, 1), 0, top)
    return jnp.take_along_axis(listing, (jnp.arange(top)[None, :] + turn) % top, axis=1)


def load_shares(count, total, reach, skew, full):
    loads = [(1 << 20) // math.isqrt(grade ** skew) + 1 for grade in range(1, count + 1)]
    largest = reach if full else min(reach, max(-(-total // count), total * loads[0] // sum(loads)))
    least = 1 if total - largest >= count - 1 else 0
    holding, rest = [largest] + [least] * (count - 1), total - largest - least * (count - 1)
    while rest > 0:
        free = [i for i in range(1, count) if holding[i] < largest] or [i for i in range(1, count) if holding[i] < reach]
        whole, budget = sum([loads[i] for i in free]), rest
        for i in free:
            extra = min(reach - holding[i], max(1, budget * loads[i] // whole), rest)
            holding[i] = holding[i] + extra
            rest = rest - extra
    return np.array(holding)


def normal_values(own_key, dims, width, most, pieces=(), held_as=jnp.bfloat16):
    entries = jax.random.normal(own_key, dims, jnp.float32) * width
    if len(pieces) > 0:
        entries = levels(own_key, dims, pieces, -0.22, 0.18) * entries
    return jnp.clip(entries, min=-most, max=most).astype(held_as)


def setup_inputs(seed: int = 0, part: int = 0) -> dict:
    key_of = jax.random.split(jax.random.key(seed), 8)
    part_keys = jax.random.split(jax.random.fold_in(key_of[7], part), 8)
    tokens = normal_values(part_keys[0], (TOKENS, D), 1.0, 6.0, ((0, 16),))
    out_grad = normal_values(part_keys[1], (TOKENS, D), 0.5, 4.0, ((0, 16),))
    expert_ids_keys = jax.random.split(jax.random.fold_in(part_keys[2], 1), TOKENS // TOK_DEV)
    expert_ids_turns = jax.random.permutation(jax.random.fold_in(part_keys[2], 3), TOKENS // TOK_DEV)
    expert_ids = jax.vmap(lambda own, number: assign_block(jax.random.fold_in(part_keys[2], 2), own, number, TOK_DEV, EXPERTS, 2, MOST, 1))(expert_ids_keys, expert_ids_turns).reshape((TOKENS, 2))
    gates = jnp.clip(0.099609375 + 0.9003906 * jax.random.uniform(part_keys[3], (TOKENS, 2), jnp.float32) ** levels(part_keys[3], (TOKENS, 2), ((0, 16),), -0.2, 0.2), 0.099609375, 1.0).astype(jnp.bfloat16)
    gate_weight = normal_values(key_of[4], (EXPERTS, D, H), D ** -0.5, 0.125, ((0, 4), (2, 4)))
    up_weight = normal_values(key_of[5], (EXPERTS, D, H), D ** -0.5, 0.125, ((0, 4), (2, 4)))
    down_weight = normal_values(key_of[6], (EXPERTS, D, H), D ** -0.5, 0.125, ((0, 4), (2, 4)))
    return dict(tokens=tokens, out_grad=out_grad, expert_ids=expert_ids, gates=gates, gate_weight=gate_weight, up_weight=up_weight, down_weight=down_weight)


row_block = 256


def swiglu_backward(rows_in, rows_grad, rows_scaled, rows_gate, weight_g, weight_u, weight_d):
    pre_gate = jnp.dot(rows_in, weight_g, preferred_element_type=jnp.float32)
    pre_up = jnp.dot(rows_in, weight_u, preferred_element_type=jnp.float32)
    back_proj = jnp.dot(rows_grad, weight_d, preferred_element_type=jnp.float32)
    sigmoid_g = jax.nn.sigmoid(pre_gate)
    activated = pre_gate * sigmoid_g
    hidden_act = activated * pre_up
    gate_part = jnp.sum(back_proj * hidden_act, axis=1)
    grad_hidden = rows_gate[:, None] * back_proj
    grad_gate_pre = (grad_hidden * pre_up * sigmoid_g * (1.0 + pre_gate * (1.0 - sigmoid_g))).astype(jnp.bfloat16)
    grad_up_pre = (grad_hidden * activated).astype(jnp.bfloat16)
    hidden_rounded = hidden_act.astype(jnp.bfloat16)
    contract_last = (((1,), (1,)), ((), ()))
    contract_first = (((0,), (0,)), ((), ()))
    input_grad = lax.dot_general(grad_gate_pre, weight_g, contract_last, preferred_element_type=jnp.float32)
    input_grad = input_grad + lax.dot_general(grad_up_pre, weight_u, contract_last, preferred_element_type=jnp.float32)
    add_gate = lax.dot_general(rows_in, grad_gate_pre, contract_first, preferred_element_type=jnp.float32)
    add_up = lax.dot_general(rows_in, grad_up_pre, contract_first, preferred_element_type=jnp.float32)
    add_down = lax.dot_general(rows_scaled, hidden_rounded, contract_first, preferred_element_type=jnp.float32)
    return input_grad, gate_part, add_gate, add_up, add_down


def group_backward(group_in, group_grad, group_ids, group_gates, gate_weight, up_weight, down_weight):
    token_count = group_in.shape[0]
    slot_count = 2 * token_count
    flat_ids = group_ids.reshape(-1).astype(jnp.int32)
    order = jnp.argsort(flat_ids, stable=True).astype(jnp.int32)
    expert_iota = jnp.arange(EXPERTS, dtype=jnp.int32)
    counts = jnp.sum((flat_ids[None, :] == expert_iota[:, None]).astype(jnp.int32), axis=1)
    starts = (jnp.cumsum(counts) - counts).astype(jnp.int32)
    order_pad = jnp.concatenate([order, jnp.full((row_block,), slot_count, jnp.int32)])
    in_ext = jnp.concatenate([group_in, jnp.zeros((1, D), jnp.bfloat16)])
    grad_ext = jnp.concatenate([group_grad, jnp.zeros((1, D), jnp.bfloat16)])
    gate_ext = jnp.concatenate([group_gates.reshape(-1).astype(jnp.float32), jnp.zeros((1,), jnp.float32)])

    def per_expert(state_now, inputs):
        weight_g, weight_u, weight_d, first, count = inputs

        def one_block(block_index, inner):
            slot_grads, slot_gates, acc_g, acc_u, acc_d = inner
            offset = (first + block_index * row_block).astype(jnp.int32)
            picked = lax.dynamic_slice_in_dim(order_pad, offset, row_block)
            inside = jnp.arange(row_block, dtype=jnp.int32) + block_index * row_block < count
            picked = jnp.where(inside, picked, slot_count).astype(jnp.int32)
            token_index = picked // 2
            rows_in = in_ext[token_index]
            rows_grad = grad_ext[token_index]
            rows_gate = gate_ext[picked]
            rows_scaled = (rows_gate[:, None] * rows_grad.astype(jnp.float32)).astype(jnp.bfloat16)
            input_grad, gate_part, add_g, add_u, add_d = swiglu_backward(rows_in, rows_grad, rows_scaled, rows_gate, weight_g, weight_u, weight_d)
            slot_grads = slot_grads.at[picked].set(input_grad.astype(jnp.bfloat16), mode="drop")
            slot_gates = slot_gates.at[picked].set(gate_part, mode="drop")
            return slot_grads, slot_gates, acc_g + add_g, acc_u + add_u, acc_d + add_d

        zero_grad = jnp.zeros((D, H), jnp.float32)
        block_total = (count + row_block - 1) // row_block
        result = lax.fori_loop(0, block_total, one_block, (state_now[0], state_now[1], zero_grad, zero_grad, zero_grad))
        return (result[0], result[1]), (result[2], result[3], result[4])

    start_state = (jnp.zeros((slot_count, D), jnp.bfloat16), jnp.zeros((slot_count,), jnp.float32))
    finals, grads = lax.scan(per_expert, start_state, (gate_weight, up_weight, down_weight, starts, counts))
    return finals[0], finals[1], grads


def reference(tokens, out_grad, expert_ids, gates, gate_weight, up_weight, down_weight):
    shaped_in = tokens.reshape(N_EXPERT, N_REPLICA, TOK_DEV, D)
    shaped_grad = out_grad.reshape(N_EXPERT, N_REPLICA, TOK_DEV, D)
    shaped_ids = expert_ids.reshape(N_EXPERT, N_REPLICA, TOK_DEV, 2)
    shaped_gates = gates.reshape(N_EXPERT, N_REPLICA, TOK_DEV, 2)
    token_parts = []
    gate_parts = []
    sums = None
    for group in range(N_REPLICA):
        slot_grads, slot_gates, grads = group_backward(
            shaped_in[:, group].reshape(-1, D), shaped_grad[:, group].reshape(-1, D),
            shaped_ids[:, group].reshape(-1, 2), shaped_gates[:, group].reshape(-1, 2),
            gate_weight, up_weight, down_weight)
        summed = slot_grads.reshape(-1, 2, D).astype(jnp.float32).sum(axis=1).astype(jnp.bfloat16)
        token_parts.append(summed.reshape(N_EXPERT, TOK_DEV, D))
        gate_parts.append(slot_gates.astype(jnp.bfloat16).reshape(N_EXPERT, TOK_DEV, 2))
        rounded = tuple(lax.optimization_barrier(member.astype(jnp.bfloat16)).astype(jnp.float32) for member in grads)
        sums = rounded if sums is None else tuple(left + right for left, right in zip(sums, rounded))
    token_grad = jnp.stack(token_parts, axis=1).reshape(TOKENS, D)
    gate_grad = jnp.stack(gate_parts, axis=1).reshape(TOKENS, 2)
    return (token_grad, gate_grad, sums[0].astype(jnp.bfloat16), sums[1].astype(jnp.bfloat16), sums[2].astype(jnp.bfloat16))
```

```python
import functools

import jax
import jax.numpy as jnp
from jax import lax
from jax.experimental import pallas as pl
from jax.experimental.pallas import tpu as pltpu
from jax.sharding import PartitionSpec as P

row_block = 256


def swiglu_backward(rows_in, rows_grad, rows_scaled, rows_gate, weight_g, weight_u, weight_d):
    pre_gate = jnp.dot(rows_in, weight_g, preferred_element_type=jnp.float32)
    pre_up = jnp.dot(rows_in, weight_u, preferred_element_type=jnp.float32)
    back_proj = jnp.dot(rows_grad, weight_d, preferred_element_type=jnp.float32)
    sigmoid_g = jax.nn.sigmoid(pre_gate)
    activated = pre_gate * sigmoid_g
    hidden_act = activated * pre_up
    gate_part = jnp.sum(back_proj * hidden_act, axis=1)
    grad_hidden = rows_gate[:, None] * back_proj
    grad_gate_pre = (
        grad_hidden * pre_up * sigmoid_g * (1.0 + pre_gate * (1.0 - sigmoid_g))
    ).astype(jnp.bfloat16)
    grad_up_pre = (grad_hidden * activated).astype(jnp.bfloat16)
    hidden_rounded = hidden_act.astype(jnp.bfloat16)
    contract_last = (((1,), (1,)), ((), ()))
    contract_first = (((0,), (0,)), ((), ()))
    input_grad = lax.dot_general(
        grad_gate_pre, weight_g, contract_last, preferred_element_type=jnp.float32
    )
    input_grad = input_grad + lax.dot_general(
        grad_up_pre, weight_u, contract_last, preferred_element_type=jnp.float32
    )
    add_gate = lax.dot_general(
        rows_in, grad_gate_pre, contract_first, preferred_element_type=jnp.float32
    )
    add_up = lax.dot_general(
        rows_in, grad_up_pre, contract_first, preferred_element_type=jnp.float32
    )
    add_down = lax.dot_general(
        rows_scaled, hidden_rounded, contract_first, preferred_element_type=jnp.float32
    )
    return (input_grad, gate_part, add_gate, add_up, add_down)


def hidden_part(state_now, pieces, first, row_data):
    gate_piece = pieces[0][0]
    up_piece = pieces[1][0]
    down_piece = pieces[2][0]
    rows_in, rows_grad, rows_scaled, rows_gate, block_total = row_data
    grad_g, grad_u, grad_d, input_acc, gate_acc = state_now
    packed = rows_in.shape[0]
    block_limit = packed // row_block

    def make_branch(block_count):
        row_total = block_count * row_block

        def branch(unused):
            input_grad, gate_part, add_g, add_u, add_d = swiglu_backward(
                rows_in[:row_total],
                rows_grad[:row_total],
                rows_scaled[:row_total],
                rows_gate[:row_total],
                gate_piece,
                up_piece,
                down_piece,
            )
            spare = packed - row_total
            input_grad = jnp.pad(input_grad, ((0, spare), (0, 0)))
            gate_part = jnp.pad(gate_part, ((0, spare),))
            return (input_grad, gate_part, add_g, add_u, add_d)

        return branch

    branches = [make_branch(count) for count in range(1, block_limit + 1)]
    which = jnp.clip(block_total - 1, 0, block_limit - 1)
    input_grad, gate_part, add_g, add_u, add_d = lax.switch(which, branches, 0)
    grad_g = lax.dynamic_update_slice_in_dim(grad_g, add_g, first, 1)
    grad_u = lax.dynamic_update_slice_in_dim(grad_u, add_u, first, 1)
    grad_d = lax.dynamic_update_slice_in_dim(grad_d, add_d, first, 1)
    return (grad_g, grad_u, grad_d, input_acc + input_grad, gate_acc + gate_part)


def general_body(tokens, out_grad, expert_ids, gates, gate_weight, up_weight, down_weight):
    tok_rows, feature_width = tokens.shape
    owners = lax.axis_size("expert")
    capacity = min(tok_rows, max(2, 6 * tok_rows // owners))
    slot_count = 2 * tok_rows
    flat_ids = expert_ids.reshape(-1)
    onehot = (flat_ids[:, None] == jnp.arange(owners, dtype=jnp.int32)[None, :]).astype(jnp.int32)
    before = jnp.cumsum(onehot, axis=0) - onehot
    position = jnp.sum(before * onehot, axis=1)
    target = flat_ids * capacity + position
    source = (
        jnp.full((owners * capacity,), slot_count, jnp.int32)
        .at[target]
        .set(jnp.arange(slot_count, dtype=jnp.int32))
    )
    in_ext = jnp.concatenate([tokens, jnp.zeros((1, feature_width), jnp.bfloat16)])
    grad_ext = jnp.concatenate([out_grad, jnp.zeros((1, feature_width), jnp.bfloat16)])
    gate_ext = jnp.concatenate([gates.reshape(-1), jnp.zeros((1,), jnp.bfloat16)])
    send_in = in_ext[source // 2].reshape(owners, capacity, feature_width)
    send_grad = grad_ext[source // 2].reshape(owners, capacity, feature_width)
    send_gate = gate_ext[source].reshape(owners, capacity)
    recv_in, recv_grad, recv_gate = (
        lax.all_to_all(send_in, "expert", split_axis=0, concat_axis=0, tiled=True),
        lax.all_to_all(send_grad, "expert", split_axis=0, concat_axis=0, tiled=True),
        lax.all_to_all(send_gate, "expert", split_axis=0, concat_axis=0, tiled=True),
    )
    recv_slots = owners * capacity
    live_rows = (recv_gate.reshape(-1) > 0).astype(jnp.int32)
    packed_pos = jnp.cumsum(live_rows) - live_rows
    live_total = jnp.sum(live_rows)
    packed = (recv_slots + row_block - 1) // row_block * row_block
    unpack = jnp.where(live_rows > 0, packed_pos, packed)
    pack_index = (
        jnp.full((packed,), recv_slots, jnp.int32)
        .at[unpack]
        .set(jnp.arange(recv_slots, dtype=jnp.int32), mode="drop")
    )
    rows_in = jnp.concatenate(
        [recv_in.reshape(recv_slots, feature_width), jnp.zeros((1, feature_width), jnp.bfloat16)]
    )[pack_index]
    rows_grad = jnp.concatenate(
        [recv_grad.reshape(recv_slots, feature_width), jnp.zeros((1, feature_width), jnp.bfloat16)]
    )[pack_index]
    rows_gate = jnp.concatenate([recv_gate.reshape(-1), jnp.zeros((1,), jnp.bfloat16)])[
        pack_index
    ].astype(jnp.float32)
    rows_scaled = (rows_gate[:, None] * rows_grad.astype(jnp.float32)).astype(jnp.bfloat16)
    block_total = (live_total + row_block - 1) // row_block
    row_data = (rows_in, rows_grad, rows_scaled, rows_gate, block_total)
    hidden_units = gate_weight.shape[2] * lax.axis_size("replica")
    zero_grad = jnp.zeros((feature_width, hidden_units), jnp.float32)
    start_state = (
        zero_grad,
        zero_grad,
        zero_grad,
        jnp.zeros((packed, feature_width), jnp.float32),
        jnp.zeros((packed,), jnp.float32),
    )
    complete = (
        lax.all_gather(gate_weight, "replica", axis=2, tiled=True),
        lax.all_gather(up_weight, "replica", axis=2, tiled=True),
        lax.all_gather(down_weight, "replica", axis=2, tiled=True),
    )
    final = hidden_part(start_state, complete, 0, row_data)
    grad_g, grad_u, grad_d, input_acc, gate_acc = final
    packed_grad = jnp.concatenate(
        [input_acc.astype(jnp.bfloat16), jnp.zeros((1, feature_width), jnp.bfloat16)]
    )
    packed_gate = jnp.concatenate([gate_acc.astype(jnp.bfloat16), jnp.zeros((1,), jnp.bfloat16)])
    back_grad = packed_grad[unpack].reshape(owners, capacity, feature_width)
    back_gate = packed_gate[unpack].reshape(owners, capacity)
    ret_grad, ret_gate = (
        lax.all_to_all(back_grad, "expert", split_axis=0, concat_axis=0, tiled=True),
        lax.all_to_all(back_gate, "expert", split_axis=0, concat_axis=0, tiled=True),
    )
    slot_grad = ret_grad.reshape(recv_slots, feature_width)[target].reshape(
        tok_rows, 2, feature_width
    )
    token_grad = slot_grad.astype(jnp.float32).sum(axis=1).astype(jnp.bfloat16)
    gate_grad = ret_gate.reshape(-1)[target].reshape(tok_rows, 2)
    shares = (
        lax.psum_scatter(
            grad_g.astype(jnp.bfloat16), "replica", scatter_dimension=1, tiled=True
        ).astype(jnp.float32),
        lax.psum_scatter(
            grad_u.astype(jnp.bfloat16), "replica", scatter_dimension=1, tiled=True
        ).astype(jnp.float32),
        lax.psum_scatter(
            grad_d.astype(jnp.bfloat16), "replica", scatter_dimension=1, tiled=True
        ).astype(jnp.float32),
    )
    return (
        token_grad,
        gate_grad,
        shares[0].astype(jnp.bfloat16)[None],
        shares[1].astype(jnp.bfloat16)[None],
        shares[2].astype(jnp.bfloat16)[None],
    )


swap_x = [(0, 2), (1, 3), (2, 0), (3, 1)]
swap_core = [(0, 1), (1, 0), (2, 3), (3, 2)]
swap_part = [(0, 1), (1, 0)]


def slot_kernel(in_ref, grad_ref, gate_ref, *rest):
    weights = rest[:12]
    gg_near, gg_far, gu_near, gu_far, hidden_send, hidden_keep, scaled_ref, back_ref = rest[12:20]
    held, total, sems = rest[20:]
    copies = []
    for share in range(4):
        for kind in range(3):
            place = share * 3 + kind
            copies.append(
                pltpu.make_async_copy(weights[place], held.at[place], sems.at[place])
            )
    for copy in copies:
        copy.start()
    rows_in = in_ref[...]
    rows_grad = grad_ref[...]
    gate = gate_ref[...]
    scaled_ref[...] = (gate * rows_grad.astype(jnp.float32)).astype(jnp.bfloat16)
    gate_sum = jnp.zeros(gate.shape, jnp.float32)
    contract_last = (((1,), (1,)), ((), ()))
    for share in range(4):
        for kind in range(3):
            copies[share * 3 + kind].wait()
        weight_g, weight_u, weight_d = held[share * 3], held[share * 3 + 1], held[share * 3 + 2]
        pre_gate = jnp.dot(rows_in, weight_g, preferred_element_type=jnp.float32)
        pre_up = jnp.dot(rows_in, weight_u, preferred_element_type=jnp.float32)
        back_proj = jnp.dot(rows_grad, weight_d, preferred_element_type=jnp.float32)
        sigmoid_g = jax.nn.sigmoid(pre_gate)
        activated = pre_gate * sigmoid_g
        hidden_act = activated * pre_up
        gate_sum = gate_sum + jnp.sum(back_proj * hidden_act, axis=1, keepdims=True)
        grad_hidden = gate * back_proj
        grad_gate = (
            grad_hidden * pre_up * sigmoid_g * (1.0 + pre_gate * (1.0 - sigmoid_g))
        ).astype(jnp.bfloat16)
        grad_up = (grad_hidden * activated).astype(jnp.bfloat16)
        width = grad_gate.shape[1]
        near_cols = slice((share % 2) * width, (share % 2 + 1) * width)
        far_cols = slice((share // 2) * width, (share // 2 + 1) * width)
        (gg_near if share < 2 else gg_far)[:, near_cols] = grad_gate
        (gu_near if share < 2 else gu_far)[:, near_cols] = grad_up
        (hidden_keep if share % 2 == 0 else hidden_send)[:, far_cols] = hidden_act.astype(
            jnp.bfloat16
        )
        part = lax.dot_general(
            grad_gate, weight_g, contract_last, preferred_element_type=jnp.float32
        ) + lax.dot_general(grad_up, weight_u, contract_last, preferred_element_type=jnp.float32)
        if share == 0:
            total[...] = part
        else:
            total[...] += part
    features = rows_in.shape[1]
    back_ref[:, :features] = total[...].astype(jnp.bfloat16)
    back_ref[:, features:] = jnp.broadcast_to(gate_sum, (gate.shape[0], 128)).astype(jnp.bfloat16)


def slot_compute(rows_in, rows_grad, gate, weights):
    rows, features = rows_in.shape
    width = weights[0].shape[1]
    bf = jnp.bfloat16
    half = jax.ShapeDtypeStruct((rows, 2 * width), bf)
    vmem = pl.BlockSpec(memory_space=pltpu.VMEM)
    return pl.pallas_call(
        slot_kernel,
        out_shape=(
            half,
            half,
            half,
            half,
            half,
            half,
            jax.ShapeDtypeStruct((rows, features), bf),
            jax.ShapeDtypeStruct((rows, features + 128), bf),
        ),
        in_specs=[vmem] * 3 + [pl.BlockSpec(memory_space=pl.ANY)] * 12,
        out_specs=(vmem,) * 8,
        scratch_shapes=[
            pltpu.VMEM((12, features, width), bf),
            pltpu.VMEM((rows, features), jnp.float32),
            pltpu.SemaphoreType.DMA((12,)),
        ],
        compiler_params=pltpu.CompilerParams(vmem_limit_bytes=44 * 1024 * 1024),
        cost_estimate=pl.CostEstimate(
            flops=40 * rows * features * width,
            bytes_accessed=24 * features * width + 10 * rows * features,
            transcendentals=4 * rows * width,
        ),
    )(rows_in, rows_grad, gate, *weights)


def chain(block, z):
    right = [(0, 1), (1, 2), (2, 3)]
    left = [(3, 2), (2, 1), (1, 0)]
    from_left = lax.ppermute(block, "expert", right)
    from_right = lax.ppermute(block, "expert", left)
    from_left2 = lax.ppermute(from_left, "expert", right[1:])
    from_right2 = lax.ppermute(from_right, "expert", left[1:])
    from_left3 = lax.ppermute(from_left2, "expert", right[2:])
    from_right3 = lax.ppermute(from_right2, "expert", left[2:])
    one = jnp.where(z % 2 == 0, from_right, from_left)
    two = jnp.where(z < 2, from_right2, from_left2)
    three = jnp.where(
        z == 0, from_right3, jnp.where(z == 1, from_right, jnp.where(z == 2, from_left, from_left3))
    )
    return one, two, three


def exchanged_weights(own, y):
    near = [lax.ppermute(w, "replica", swap_core) for w in own]
    half = own[0].shape[0] // 2
    far = []
    for w in own:
        mine = lax.dynamic_slice_in_dim(w, y * half, half, 0)
        across = lax.ppermute(mine, "replica", swap_x)
        other = lax.ppermute(across, "parts", swap_part)
        far.append(
            jnp.concatenate([jnp.where(y == 0, across, other), jnp.where(y == 0, other, across)])
        )
    far_near = [lax.ppermute(w, "replica", swap_core) for w in far]
    return near, far, far_near


def fast_body(tokens, out_grad, expert_ids, gates, gate_weight, up_weight, down_weight):
    z = lax.axis_index("expert")
    y = lax.axis_index("parts")
    rows, features = tokens.shape
    gates_wide = gates.astype(jnp.float32)
    experts = [z ^ step for step in range(4)]
    gate_to = [
        jnp.sum(jnp.where(expert_ids == e, gates_wide, 0.0), axis=1, keepdims=True) for e in experts
    ]
    slot_gate = [gate_to[0]] + [
        lax.ppermute(
            gate_to[step].astype(jnp.bfloat16).reshape(1, rows),
            "expert",
            [(i, i ^ step) for i in range(4)],
        )
        .astype(jnp.float32)
        .reshape(rows, 1)
        for step in (1, 2, 3)
    ]
    own = [gate_weight[0], up_weight[0], down_weight[0]]
    near, far, far_near = exchanged_weights(own, y)
    weights = own + near + far + far_near
    slot_in = [tokens, *chain(tokens, z)]
    slot_grad = [out_grad, *chain(out_grad, z)]
    groups = ((0, 1), (2,), (3,))

    def joined(parts):
        return parts[0] if len(parts) == 1 else jnp.concatenate(parts)

    results = []
    group_in = []
    for group in groups:
        g_in = joined([slot_in[i] for i in group])
        group_in.append(g_in)
        results.append(
            slot_compute(
                g_in,
                joined([slot_grad[i] for i in group]),
                joined([slot_gate[i] for i in group]),
                weights,
            )
        )
    gg_near, gg_far, gu_near, gu_far, hidden_send, hidden_keep, scaled, _ = (
        jnp.concatenate([r[i] for r in results]) if i < 7 else None for i in range(8)
    )
    rows_all = jnp.concatenate(group_in)
    backs = []
    for group, result in zip(groups, results):
        for place, _ in enumerate(group):
            backs.append(result[7][place * rows : (place + 1) * rows])
    returned = [backs[0]] + [
        lax.ppermute(backs[step], "expert", [(i, i ^ step) for i in range(4)]) for step in (1, 2, 3)
    ]
    contract_first = (((0,), (0,)), ((), ()))

    def outer(lhs, rhs):
        return lax.dot_general(
            lhs, rhs, contract_first, preferred_element_type=jnp.float32
        ).astype(jnp.bfloat16)

    width = own[0].shape[1]

    def reduced(send, keep):
        got = lax.ppermute(send, "replica", swap_core)
        both = keep.astype(jnp.float32) + got.astype(jnp.float32)
        crossing = lax.ppermute(both[:, width:].astype(jnp.bfloat16), "replica", swap_x)
        return (both[:, :width] + crossing.astype(jnp.float32)).astype(jnp.bfloat16)

    def columns(near_part, far_part, pick):
        cols = slice(pick * width, (pick + 1) * width)
        return jnp.concatenate([near_part[:, cols], far_part[:, cols]], axis=1)

    down = reduced(outer(scaled, hidden_send), outer(scaled, hidden_keep))
    gate_out = reduced(
        outer(rows_all, columns(gg_near, gg_far, 1)), outer(rows_all, columns(gg_near, gg_far, 0))
    )
    up_out = reduced(
        outer(rows_all, columns(gu_near, gu_far, 1)), outer(rows_all, columns(gu_near, gu_far, 0))
    )
    token_grad = sum(r[:, :features].astype(jnp.float32) for r in returned).astype(jnp.bfloat16)
    gate_grad = sum(
        jnp.where(expert_ids == e, r[:, features : features + 1].astype(jnp.float32), 0.0)
        for e, r in zip(experts, returned)
    ).astype(jnp.bfloat16)
    return token_grad, gate_grad, gate_out[None], up_out[None], down[None]


def body(*args):
    sizes = tuple(lax.axis_size(name) for name in ("parts", "expert", "replica"))
    if sizes == (2, 4, 4):
        return fast_body(*args)
    return general_body(*args)


def solution(mesh):
    in_specs = (
        P(("parts", "expert", "replica"), None),
        P(("parts", "expert", "replica"), None),
        P(("parts", "expert", "replica"), None),
        P(("parts", "expert", "replica"), None),
        P("expert", None, "replica"),
        P("expert", None, "replica"),
        P("expert", None, "replica"),
    )
    out_specs = (
        P(("parts", "expert", "replica"), None),
        P(("parts", "expert", "replica"), None),
        P(("parts", "expert"), None, "replica"),
        P(("parts", "expert"), None, "replica"),
        P(("parts", "expert"), None, "replica"),
    )
    return jax.shard_map(body, mesh=mesh, in_specs=in_specs, out_specs=out_specs, check_vma=False)
```

```python
import functools

import jax
import jax.numpy as jnp
from jax import lax
from jax.experimental import pallas as pl
from jax.experimental.pallas import tpu as pltpu
from jax.sharding import PartitionSpec as P

row_block = 256


def swiglu_backward(rows_in, rows_grad, rows_scaled, rows_gate, weight_g, weight_u, weight_d):
    pre_gate = jnp.dot(rows_in, weight_g, preferred_element_type=jnp.float32)
    pre_up = jnp.dot(rows_in, weight_u, preferred_element_type=jnp.float32)
    back_proj = jnp.dot(rows_grad, weight_d, preferred_element_type=jnp.float32)
    sigmoid_g = jax.nn.sigmoid(pre_gate)
    activated = pre_gate * sigmoid_g
    hidden_act = activated * pre_up
    gate_part = jnp.sum(back_proj * hidden_act, axis=1)
    grad_hidden = rows_gate[:, None] * back_proj
    grad_gate_pre = (
        grad_hidden * pre_up * sigmoid_g * (1.0 + pre_gate * (1.0 - sigmoid_g))
    ).astype(jnp.bfloat16)
    grad_up_pre = (grad_hidden * activated).astype(jnp.bfloat16)
    hidden_rounded = hidden_act.astype(jnp.bfloat16)
    contract_last = (((1,), (1,)), ((), ()))
    contract_first = (((0,), (0,)), ((), ()))
    input_grad = lax.dot_general(
        grad_gate_pre, weight_g, contract_last, preferred_element_type=jnp.float32
    )
    input_grad = input_grad + lax.dot_general(
        grad_up_pre, weight_u, contract_last, preferred_element_type=jnp.float32
    )
    add_gate = lax.dot_general(
        rows_in, grad_gate_pre, contract_first, preferred_element_type=jnp.float32
    )
    add_up = lax.dot_general(
        rows_in, grad_up_pre, contract_first, preferred_element_type=jnp.float32
    )
    add_down = lax.dot_general(
        rows_scaled, hidden_rounded, contract_first, preferred_element_type=jnp.float32
    )
    return (input_grad, gate_part, add_gate, add_up, add_down)


def hidden_part(state_now, pieces, first, row_data):
    gate_piece = pieces[0][0]
    up_piece = pieces[1][0]
    down_piece = pieces[2][0]
    rows_in, rows_grad, rows_scaled, rows_gate, block_total = row_data
    grad_g, grad_u, grad_d, input_acc, gate_acc = state_now
    packed = rows_in.shape[0]
    block_limit = packed // row_block

    def make_branch(block_count):
        row_total = block_count * row_block

        def branch(unused):
            input_grad, gate_part, add_g, add_u, add_d = swiglu_backward(
                rows_in[:row_total],
                rows_grad[:row_total],
                rows_scaled[:row_total],
                rows_gate[:row_total],
                gate_piece,
                up_piece,
                down_piece,
            )
            spare = packed - row_total
            input_grad = jnp.pad(input_grad, ((0, spare), (0, 0)))
            gate_part = jnp.pad(gate_part, ((0, spare),))
            return (input_grad, gate_part, add_g, add_u, add_d)

        return branch

    branches = [make_branch(count) for count in range(1, block_limit + 1)]
    which = jnp.clip(block_total - 1, 0, block_limit - 1)
    input_grad, gate_part, add_g, add_u, add_d = lax.switch(which, branches, 0)
    grad_g = lax.dynamic_update_slice_in_dim(grad_g, add_g, first, 1)
    grad_u = lax.dynamic_update_slice_in_dim(grad_u, add_u, first, 1)
    grad_d = lax.dynamic_update_slice_in_dim(grad_d, add_d, first, 1)
    return (grad_g, grad_u, grad_d, input_acc + input_grad, gate_acc + gate_part)


def general_body(tokens, out_grad, expert_ids, gates, gate_weight, up_weight, down_weight):
    tok_rows, feature_width = tokens.shape
    owners = lax.axis_size("expert")
    capacity = min(tok_rows, max(2, 6 * tok_rows // owners))
    slot_count = 2 * tok_rows
    flat_ids = expert_ids.reshape(-1)
    onehot = (flat_ids[:, None] == jnp.arange(owners, dtype=jnp.int32)[None, :]).astype(jnp.int32)
    before = jnp.cumsum(onehot, axis=0) - onehot
    position = jnp.sum(before * onehot, axis=1)
    target = flat_ids * capacity + position
    source = (
        jnp.full((owners * capacity,), slot_count, jnp.int32)
        .at[target]
        .set(jnp.arange(slot_count, dtype=jnp.int32))
    )
    in_ext = jnp.concatenate([tokens, jnp.zeros((1, feature_width), jnp.bfloat16)])
    grad_ext = jnp.concatenate([out_grad, jnp.zeros((1, feature_width), jnp.bfloat16)])
    gate_ext = jnp.concatenate([gates.reshape(-1), jnp.zeros((1,), jnp.bfloat16)])
    send_in = in_ext[source // 2].reshape(owners, capacity, feature_width)
    send_grad = grad_ext[source // 2].reshape(owners, capacity, feature_width)
    send_gate = gate_ext[source].reshape(owners, capacity)
    recv_in, recv_grad, recv_gate = (
        lax.all_to_all(send_in, "expert", split_axis=0, concat_axis=0, tiled=True),
        lax.all_to_all(send_grad, "expert", split_axis=0, concat_axis=0, tiled=True),
        lax.all_to_all(send_gate, "expert", split_axis=0, concat_axis=0, tiled=True),
    )
    recv_slots = owners * capacity
    live_rows = (recv_gate.reshape(-1) > 0).astype(jnp.int32)
    packed_pos = jnp.cumsum(live_rows) - live_rows
    live_total = jnp.sum(live_rows)
    packed = (recv_slots + row_block - 1) // row_block * row_block
    unpack = jnp.where(live_rows > 0, packed_pos, packed)
    pack_index = (
        jnp.full((packed,), recv_slots, jnp.int32)
        .at[unpack]
        .set(jnp.arange(recv_slots, dtype=jnp.int32), mode="drop")
    )
    rows_in = jnp.concatenate(
        [recv_in.reshape(recv_slots, feature_width), jnp.zeros((1, feature_width), jnp.bfloat16)]
    )[pack_index]
    rows_grad = jnp.concatenate(
        [recv_grad.reshape(recv_slots, feature_width), jnp.zeros((1, feature_width), jnp.bfloat16)]
    )[pack_index]
    rows_gate = jnp.concatenate([recv_gate.reshape(-1), jnp.zeros((1,), jnp.bfloat16)])[
        pack_index
    ].astype(jnp.float32)
    rows_scaled = (rows_gate[:, None] * rows_grad.astype(jnp.float32)).astype(jnp.bfloat16)
    block_total = (live_total + row_block - 1) // row_block
    row_data = (rows_in, rows_grad, rows_scaled, rows_gate, block_total)
    hidden_units = gate_weight.shape[2] * lax.axis_size("replica")
    zero_grad = jnp.zeros((feature_width, hidden_units), jnp.float32)
    start_state = (
        zero_grad,
        zero_grad,
        zero_grad,
        jnp.zeros((packed, feature_width), jnp.float32),
        jnp.zeros((packed,), jnp.float32),
    )
    complete = (
        lax.all_gather(gate_weight, "replica", axis=2, tiled=True),
        lax.all_gather(up_weight, "replica", axis=2, tiled=True),
        lax.all_gather(down_weight, "replica", axis=2, tiled=True),
    )
    final = hidden_part(start_state, complete, 0, row_data)
    grad_g, grad_u, grad_d, input_acc, gate_acc = final
    packed_grad = jnp.concatenate(
        [input_acc.astype(jnp.bfloat16), jnp.zeros((1, feature_width), jnp.bfloat16)]
    )
    packed_gate = jnp.concatenate([gate_acc.astype(jnp.bfloat16), jnp.zeros((1,), jnp.bfloat16)])
    back_grad = packed_grad[unpack].reshape(owners, capacity, feature_width)
    back_gate = packed_gate[unpack].reshape(owners, capacity)
    ret_grad, ret_gate = (
        lax.all_to_all(back_grad, "expert", split_axis=0, concat_axis=0, tiled=True),
        lax.all_to_all(back_gate, "expert", split_axis=0, concat_axis=0, tiled=True),
    )
    slot_grad = ret_grad.reshape(recv_slots, feature_width)[target].reshape(
        tok_rows, 2, feature_width
    )
    token_grad = slot_grad.astype(jnp.float32).sum(axis=1).astype(jnp.bfloat16)
    gate_grad = ret_gate.reshape(-1)[target].reshape(tok_rows, 2)
    shares = (
        lax.psum_scatter(
            grad_g.astype(jnp.bfloat16), "replica", scatter_dimension=1, tiled=True
        ).astype(jnp.float32),
        lax.psum_scatter(
            grad_u.astype(jnp.bfloat16), "replica", scatter_dimension=1, tiled=True
        ).astype(jnp.float32),
        lax.psum_scatter(
            grad_d.astype(jnp.bfloat16), "replica", scatter_dimension=1, tiled=True
        ).astype(jnp.float32),
    )
    return (
        token_grad,
        gate_grad,
        shares[0].astype(jnp.bfloat16)[None],
        shares[1].astype(jnp.bfloat16)[None],
        shares[2].astype(jnp.bfloat16)[None],
    )


swap_x = [(0, 2), (1, 3), (2, 0), (3, 1)]
swap_core = [(0, 1), (1, 0), (2, 3), (3, 2)]
swap_part = [(0, 1), (1, 0)]


def slot_kernel(slots, lane_ref, part_ref, *rest):
    ins, grads, rest = rest[:slots], rest[slots : 2 * slots], rest[2 * slots :]
    own, near, far, far_near = rest[:3], rest[3], rest[4:8], rest[8:12]
    near_ref, far_ref, hidden_send, hidden_keep, scaled_ref = rest[12:17]
    backs, rest = rest[17 : 17 + slots], rest[17 + slots :]
    held, held_down, rows_in, rows_grad, acts, sems = rest
    features = held.shape[0]
    width = held.shape[1] // 8
    half, quarter = features // 2, features // 4
    copies = [[] for _ in range(4)]
    first = pl.multiple_of(part_ref[0] * half, half)
    second = pl.multiple_of(half - part_ref[0] * half, half)
    count = 0
    for share, (group, lines) in enumerate(
        ((own, None), (near, None), (far, (first, second)), (far_near, (first, second)))
    ):
        for kind in range(3):
            target = held_down if kind == 2 else held
            column = share * width if kind == 2 else (2 * share + kind) * width
            columns = pl.ds(column, width)
            if share == 0:
                pairs = [(own[kind], target.at[:, columns])]
            elif share == 1:
                pairs = [(near.at[kind], target.at[:, columns])]
            else:
                pairs = [
                    (group[2 * side + kind // 2].at[kind % 2], target.at[pl.ds(line, half), columns])
                    for side, line in enumerate(lines)
                ]
            for source, place in pairs:
                copies[share].append(pltpu.make_async_copy(source, place, sems.at[count]))
                count += 1
    for group in copies:
        for copy in group:
            copy.start()
    height = ins[0].shape[0]
    gates = []
    for slot, (in_ref, grad_ref) in enumerate(zip(ins, grads)):
        lines = slice(slot * height, (slot + 1) * height)
        rows_in[lines, :] = in_ref[...]
        rows_grad[lines, :] = grad_ref[:, :features]
        lanes = grad_ref[:, features:].astype(jnp.float32)
        gates.append(jnp.sum(lanes * lane_ref[...], axis=1, keepdims=True))
    gate = jnp.concatenate(gates)
    scaled_ref[...] = (gate * rows_grad[...].astype(jnp.float32)).astype(jnp.bfloat16)
    gate_sum = jnp.zeros(gate.shape, jnp.float32)
    for share in range(4):
        for copy in copies[share]:
            copy.wait()
        both = slice(2 * share * width, 2 * (share + 1) * width)
        pre = jnp.dot(rows_in[...], held[:, both], preferred_element_type=jnp.float32)
        pre_gate, pre_up = pre[:, :width], pre[:, width:]
        back_proj = jnp.dot(
            rows_grad[...],
            held_down[:, share * width : (share + 1) * width],
            preferred_element_type=jnp.float32,
        )
        sigmoid_g = jax.nn.sigmoid(pre_gate)
        activated = pre_gate * sigmoid_g
        hidden_act = activated * pre_up
        gate_sum = gate_sum + jnp.sum(back_proj * hidden_act, axis=1, keepdims=True)
        grad_hidden = gate * back_proj
        grad_gate = (
            grad_hidden * pre_up * sigmoid_g * (1.0 + pre_gate * (1.0 - sigmoid_g))
        ).astype(jnp.bfloat16)
        grad_up = (grad_hidden * activated).astype(jnp.bfloat16)
        acts[:, 2 * share * width : (2 * share + 1) * width] = grad_gate
        acts[:, (2 * share + 1) * width : 2 * (share + 1) * width] = grad_up
        hidden = hidden_send if share % 2 else hidden_keep
        pick = share // 2
        hidden[:, pick * width : (pick + 1) * width] = hidden_act.astype(jnp.bfloat16)
    near_ref[...] = acts[:, : 4 * width]
    far_ref[...] = acts[:, 4 * width :]
    for piece in range(4):
        lines = slice(piece * quarter, (piece + 1) * quarter)
        part = lax.dot_general(
            acts[...],
            held[lines, :],
            (((1,), (1,)), ((), ())),
            preferred_element_type=jnp.float32,
        ).astype(jnp.bfloat16)
        for slot, back in enumerate(backs):
            back[:, lines] = part[slot * height : (slot + 1) * height]
    for slot, back in enumerate(backs):
        back[:, features:] = jnp.broadcast_to(
            gate_sum[slot * height : (slot + 1) * height], (height, 128)
        ).astype(jnp.bfloat16)


def slot_compute(ins, grads, lane, part, weights):
    slots = len(ins)
    height = ins[0].shape[0]
    rows = slots * height
    features, width = weights[0].shape
    bf = jnp.bfloat16
    shapes = [(rows, c) for c in (4 * width, 4 * width, 2 * width, 2 * width, features)]
    shapes += [(height, features + 128)] * slots
    vmem = pl.BlockSpec(memory_space=pltpu.VMEM)
    out = pl.pallas_call(
        functools.partial(slot_kernel, slots),
        out_shape=[jax.ShapeDtypeStruct(shape, bf) for shape in shapes],
        in_specs=[vmem, pl.BlockSpec(memory_space=pltpu.SMEM)]
        + [vmem] * (2 * slots)
        + [pl.BlockSpec(memory_space=pl.ANY)] * 12,
        out_specs=[vmem] * len(shapes),
        scratch_shapes=[
            pltpu.VMEM((features, 8 * width), bf),
            pltpu.VMEM((features, 4 * width), bf),
            pltpu.VMEM((rows, features), bf),
            pltpu.VMEM((rows, features), bf),
            pltpu.VMEM((rows, 8 * width), bf),
            pltpu.SemaphoreType.DMA((18,)),
        ],
        compiler_params=pltpu.CompilerParams(vmem_limit_bytes=48 * 1024 * 1024),
        cost_estimate=pl.CostEstimate(
            flops=rows * features, bytes_accessed=2 * rows * features, transcendentals=0
        ),
    )(lane, part, *ins, *grads, *weights)
    return (*out[:5], out[5:])


def tied(*values):
    return lax.optimization_barrier(values)


def over_z(value, pairs):
    return lax.ppermute(value, "expert", pairs)


def over_x(value):
    return lax.ppermute(value, "replica", swap_x)


def over_core(value):
    return lax.ppermute(value, "replica", swap_core)


def over_parts(value):
    return lax.ppermute(value, "parts", swap_part)


def apart(step):
    return [(i, i ^ step) for i in range(4)]


def outer(lhs, rhs):
    return lax.dot_general(lhs, rhs, (((0,), (0,)), ((), ())), preferred_element_type=jnp.float32)


def fast_body(tokens, out_grad, expert_ids, gates, gate_weight, up_weight, down_weight):
    z = lax.axis_index("expert")
    y = lax.axis_index("parts")
    rows, features = tokens.shape
    bf, f32 = jnp.bfloat16, jnp.float32
    half = features // 2
    own = [gate_weight[0], up_weight[0], down_weight[0]]
    width = own[0].shape[1]
    halves = [lax.dynamic_slice_in_dim(w, y * half, half, 0) for w in own]
    pieces = [jnp.stack(halves[:2]), halves[2][None]]
    lanes = jnp.arange(128, dtype=jnp.int32)[None, :]
    gate_lanes = sum(
        jnp.where(expert_ids[:, k : k + 1] == lanes, gates[:, k : k + 1], 0) for k in range(2)
    ).astype(bf)
    lane = (lanes == z).astype(f32)
    wide_grad = jnp.concatenate([out_grad, gate_lanes], axis=1)
    part_index = jnp.reshape(y, (1,)).astype(jnp.int32)

    in_two, in_one = over_z(tokens, apart(2)), over_z(tokens, apart(1))
    across_0 = over_x(pieces[0])
    in_two, in_one, across_0, wide_grad, tokens_x, piece_1, stacked = tied(
        in_two, in_one, across_0, wide_grad, tokens, pieces[1], jnp.stack(own)
    )

    grad_two, grad_one = over_z(wide_grad, apart(2)), over_z(wide_grad, apart(1))
    across_1 = over_x(piece_1)
    other_0 = over_parts(across_0)
    near = over_core(stacked)
    across_1, near, tokens_x = tied(across_1, near, tokens_x)
    other_1 = over_parts(across_1)
    far_a = over_x(tokens_x)
    in_bc = jnp.concatenate([in_one, in_two])
    two = jnp.concatenate([in_two, grad_two], axis=1)
    two, grad_one, in_bc, far_a, across_0, across_1, other_0, other_1 = tied(
        two, grad_one, in_bc, far_a, across_0, across_1, other_0, other_1
    )

    three = over_z(two, apart(1))
    far_bc = over_x(in_bc)
    far_weights = [across_0, across_1, other_0, other_1]
    weights = [*own, near, *far_weights, *[over_core(w) for w in far_weights]]
    acts_abc, crossing_abc, send_abc, keep_abc, scaled_abc, backs = slot_compute(
        [tokens, in_one, in_two], [wide_grad, grad_one, grad_two], lane, part_index, weights
    )
    three, far_bc, crossing_abc, back_a, back_b, back_c = tied(three, far_bc, crossing_abc, *backs)

    in_d, grad_d = three[:, :features], three[:, features:]
    far_d = over_x(in_d)
    back_one = over_z(back_b, apart(1))
    acts_d, crossing_d, send_d, keep_d, scaled_d, (back_d,) = slot_compute(
        [in_d], [grad_d], lane, part_index, weights
    )
    far_d, back_one, acts_d, crossing_d, send_d, keep_d, scaled_d, back_d, back_c = tied(
        far_d, back_one, acts_d, crossing_d, send_d, keep_d, scaled_d, back_d, back_c
    )

    acts_far = over_x(jnp.concatenate([crossing_abc, crossing_d]))
    back_two = over_z(back_c, apart(2))
    scaled = jnp.concatenate([scaled_abc, scaled_d])
    send = outer(scaled, jnp.concatenate([send_abc, send_d])).astype(bf)
    keep = outer(scaled, jnp.concatenate([keep_abc, keep_d])).astype(bf)
    both = keep.astype(f32) + over_core(send).astype(f32)
    acts = jnp.concatenate([acts_abc, acts_d])
    rows_near = jnp.concatenate([tokens, in_bc, in_d])
    part_keep = outer(rows_near, acts[:, : 2 * width]).astype(bf)
    part_send = outer(rows_near, acts[:, 2 * width :]).astype(bf)
    rows_far = jnp.concatenate([far_a, far_bc, far_d])
    crossing, both = both[:, width:].astype(bf), both[:, :width]
    acts_far, back_two, crossing, both, part_keep, part_send, rows_far, back_d = tied(
        acts_far, back_two, crossing, both, part_keep, part_send, rows_far, back_d
    )

    down_far = over_x(crossing)
    back_three = over_z(back_d, apart(3))
    part_send = part_send.astype(f32) + outer(rows_far, acts_far[:, 2 * width :])
    part_keep = part_keep.astype(f32) + outer(rows_far, acts_far[:, : 2 * width])
    pair = (part_keep + over_core(part_send.astype(bf)).astype(f32)).astype(bf)
    gate_out, up_out = pair[:, :width], pair[:, width:]
    back_three, down_far, gate_out, up_out = tied(back_three, down_far, gate_out, up_out)
    returned = [back_a, back_one, back_two, back_three]
    down = (both + down_far.astype(f32)).astype(bf)
    token_grad = sum(r[:, :features].astype(f32) for r in returned).astype(bf)
    gate_grad = sum(
        jnp.where(expert_ids == (z ^ step), r[:, features : features + 1].astype(f32), 0.0)
        for step, r in enumerate(returned)
    ).astype(bf)
    return token_grad, gate_grad, gate_out[None], up_out[None], down[None]


def body(*args):
    sizes = tuple(lax.axis_size(name) for name in ("parts", "expert", "replica"))
    if sizes == (2, 4, 4):
        return fast_body(*args)
    return general_body(*args)


def solution(mesh):
    in_specs = (
        P(("parts", "expert", "replica"), None),
        P(("parts", "expert", "replica"), None),
        P(("parts", "expert", "replica"), None),
        P(("parts", "expert", "replica"), None),
        P("expert", None, "replica"),
        P("expert", None, "replica"),
        P("expert", None, "replica"),
    )
    out_specs = (
        P(("parts", "expert", "replica"), None),
        P(("parts", "expert", "replica"), None),
        P(("parts", "expert"), None, "replica"),
        P(("parts", "expert"), None, "replica"),
        P(("parts", "expert"), None, "replica"),
    )
    return jax.shard_map(body, mesh=mesh, in_specs=in_specs, out_specs=out_specs, check_vma=False)
```

```python
import functools

import jax
import jax.numpy as jnp
from jax import lax
from jax.experimental import pallas as pl
from jax.experimental.pallas import tpu as pltpu
from jax.sharding import PartitionSpec as P

row_block = 256


def swiglu_backward(rows_in, rows_grad, rows_scaled, rows_gate, weight_g, weight_u, weight_d):
    pre_gate = jnp.dot(rows_in, weight_g, preferred_element_type=jnp.float32)
    pre_up = jnp.dot(rows_in, weight_u, preferred_element_type=jnp.float32)
    back_proj = jnp.dot(rows_grad, weight_d, preferred_element_type=jnp.float32)
    sigmoid_g = jax.nn.sigmoid(pre_gate)
    activated = pre_gate * sigmoid_g
    hidden_act = activated * pre_up
    gate_part = jnp.sum(back_proj * hidden_act, axis=1)
    grad_hidden = rows_gate[:, None] * back_proj
    grad_gate_pre = (
        grad_hidden * pre_up * sigmoid_g * (1.0 + pre_gate * (1.0 - sigmoid_g))
    ).astype(jnp.bfloat16)
    grad_up_pre = (grad_hidden * activated).astype(jnp.bfloat16)
    hidden_rounded = hidden_act.astype(jnp.bfloat16)
    contract_last = (((1,), (1,)), ((), ()))
    contract_first = (((0,), (0,)), ((), ()))
    input_grad = lax.dot_general(
        grad_gate_pre, weight_g, contract_last, preferred_element_type=jnp.float32
    )
    input_grad = input_grad + lax.dot_general(
        grad_up_pre, weight_u, contract_last, preferred_element_type=jnp.float32
    )
    add_gate = lax.dot_general(
        rows_in, grad_gate_pre, contract_first, preferred_element_type=jnp.float32
    )
    add_up = lax.dot_general(
        rows_in, grad_up_pre, contract_first, preferred_element_type=jnp.float32
    )
    add_down = lax.dot_general(
        rows_scaled, hidden_rounded, contract_first, preferred_element_type=jnp.float32
    )
    return (input_grad, gate_part, add_gate, add_up, add_down)


def hidden_part(state_now, pieces, first, row_data):
    gate_piece = pieces[0][0]
    up_piece = pieces[1][0]
    down_piece = pieces[2][0]
    rows_in, rows_grad, rows_scaled, rows_gate, block_total = row_data
    grad_g, grad_u, grad_d, input_acc, gate_acc = state_now
    packed = rows_in.shape[0]
    block_limit = packed // row_block

    def make_branch(block_count):
        row_total = block_count * row_block

        def branch(unused):
            input_grad, gate_part, add_g, add_u, add_d = swiglu_backward(
                rows_in[:row_total],
                rows_grad[:row_total],
                rows_scaled[:row_total],
                rows_gate[:row_total],
                gate_piece,
                up_piece,
                down_piece,
            )
            spare = packed - row_total
            input_grad = jnp.pad(input_grad, ((0, spare), (0, 0)))
            gate_part = jnp.pad(gate_part, ((0, spare),))
            return (input_grad, gate_part, add_g, add_u, add_d)

        return branch

    branches = [make_branch(count) for count in range(1, block_limit + 1)]
    which = jnp.clip(block_total - 1, 0, block_limit - 1)
    input_grad, gate_part, add_g, add_u, add_d = lax.switch(which, branches, 0)
    grad_g = lax.dynamic_update_slice_in_dim(grad_g, add_g, first, 1)
    grad_u = lax.dynamic_update_slice_in_dim(grad_u, add_u, first, 1)
    grad_d = lax.dynamic_update_slice_in_dim(grad_d, add_d, first, 1)
    return (grad_g, grad_u, grad_d, input_acc + input_grad, gate_acc + gate_part)


def general_body(tokens, out_grad, expert_ids, gates, gate_weight, up_weight, down_weight):
    tok_rows, feature_width = tokens.shape
    owners = lax.axis_size("expert")
    capacity = min(tok_rows, max(2, 6 * tok_rows // owners))
    slot_count = 2 * tok_rows
    flat_ids = expert_ids.reshape(-1)
    onehot = (flat_ids[:, None] == jnp.arange(owners, dtype=jnp.int32)[None, :]).astype(jnp.int32)
    before = jnp.cumsum(onehot, axis=0) - onehot
    position = jnp.sum(before * onehot, axis=1)
    target = flat_ids * capacity + position
    source = (
        jnp.full((owners * capacity,), slot_count, jnp.int32)
        .at[target]
        .set(jnp.arange(slot_count, dtype=jnp.int32))
    )
    in_ext = jnp.concatenate([tokens, jnp.zeros((1, feature_width), jnp.bfloat16)])
    grad_ext = jnp.concatenate([out_grad, jnp.zeros((1, feature_width), jnp.bfloat16)])
    gate_ext = jnp.concatenate([gates.reshape(-1), jnp.zeros((1,), jnp.bfloat16)])
    send_in = in_ext[source // 2].reshape(owners, capacity, feature_width)
    send_grad = grad_ext[source // 2].reshape(owners, capacity, feature_width)
    send_gate = gate_ext[source].reshape(owners, capacity)
    recv_in, recv_grad, recv_gate = (
        lax.all_to_all(send_in, "expert", split_axis=0, concat_axis=0, tiled=True),
        lax.all_to_all(send_grad, "expert", split_axis=0, concat_axis=0, tiled=True),
        lax.all_to_all(send_gate, "expert", split_axis=0, concat_axis=0, tiled=True),
    )
    recv_slots = owners * capacity
    live_rows = (recv_gate.reshape(-1) > 0).astype(jnp.int32)
    packed_pos = jnp.cumsum(live_rows) - live_rows
    live_total = jnp.sum(live_rows)
    packed = (recv_slots + row_block - 1) // row_block * row_block
    unpack = jnp.where(live_rows > 0, packed_pos, packed)
    pack_index = (
        jnp.full((packed,), recv_slots, jnp.int32)
        .at[unpack]
        .set(jnp.arange(recv_slots, dtype=jnp.int32), mode="drop")
    )
    rows_in = jnp.concatenate(
        [recv_in.reshape(recv_slots, feature_width), jnp.zeros((1, feature_width), jnp.bfloat16)]
    )[pack_index]
    rows_grad = jnp.concatenate(
        [recv_grad.reshape(recv_slots, feature_width), jnp.zeros((1, feature_width), jnp.bfloat16)]
    )[pack_index]
    rows_gate = jnp.concatenate([recv_gate.reshape(-1), jnp.zeros((1,), jnp.bfloat16)])[
        pack_index
    ].astype(jnp.float32)
    rows_scaled = (rows_gate[:, None] * rows_grad.astype(jnp.float32)).astype(jnp.bfloat16)
    block_total = (live_total + row_block - 1) // row_block
    row_data = (rows_in, rows_grad, rows_scaled, rows_gate, block_total)
    hidden_units = gate_weight.shape[2] * lax.axis_size("replica")
    zero_grad = jnp.zeros((feature_width, hidden_units), jnp.float32)
    start_state = (
        zero_grad,
        zero_grad,
        zero_grad,
        jnp.zeros((packed, feature_width), jnp.float32),
        jnp.zeros((packed,), jnp.float32),
    )
    complete = (
        lax.all_gather(gate_weight, "replica", axis=2, tiled=True),
        lax.all_gather(up_weight, "replica", axis=2, tiled=True),
        lax.all_gather(down_weight, "replica", axis=2, tiled=True),
    )
    final = hidden_part(start_state, complete, 0, row_data)
    grad_g, grad_u, grad_d, input_acc, gate_acc = final
    packed_grad = jnp.concatenate(
        [input_acc.astype(jnp.bfloat16), jnp.zeros((1, feature_width), jnp.bfloat16)]
    )
    packed_gate = jnp.concatenate([gate_acc.astype(jnp.bfloat16), jnp.zeros((1,), jnp.bfloat16)])
    back_grad = packed_grad[unpack].reshape(owners, capacity, feature_width)
    back_gate = packed_gate[unpack].reshape(owners, capacity)
    ret_grad, ret_gate = (
        lax.all_to_all(back_grad, "expert", split_axis=0, concat_axis=0, tiled=True),
        lax.all_to_all(back_gate, "expert", split_axis=0, concat_axis=0, tiled=True),
    )
    slot_grad = ret_grad.reshape(recv_slots, feature_width)[target].reshape(
        tok_rows, 2, feature_width
    )
    token_grad = slot_grad.astype(jnp.float32).sum(axis=1).astype(jnp.bfloat16)
    gate_grad = ret_gate.reshape(-1)[target].reshape(tok_rows, 2)
    shares = (
        lax.psum_scatter(
            grad_g.astype(jnp.bfloat16), "replica", scatter_dimension=1, tiled=True
        ).astype(jnp.float32),
        lax.psum_scatter(
            grad_u.astype(jnp.bfloat16), "replica", scatter_dimension=1, tiled=True
        ).astype(jnp.float32),
        lax.psum_scatter(
            grad_d.astype(jnp.bfloat16), "replica", scatter_dimension=1, tiled=True
        ).astype(jnp.float32),
    )
    return (
        token_grad,
        gate_grad,
        shares[0].astype(jnp.bfloat16)[None],
        shares[1].astype(jnp.bfloat16)[None],
        shares[2].astype(jnp.bfloat16)[None],
    )


swap_x = [(0, 2), (1, 3), (2, 0), (3, 1)]
swap_core = [(0, 1), (1, 0), (2, 3), (3, 2)]
swap_part = [(0, 1), (1, 0)]


def slot_kernel(slots, lane_ref, part_ref, *rest):
    ins, grads, rest = rest[:slots], rest[slots : 2 * slots], rest[2 * slots :]
    own, near, far, far_near = rest[:3], rest[3], rest[4:10], rest[10:16]
    near_ref, far_ref, hidden_send, hidden_keep, scaled_ref = rest[16:21]
    backs, rest = rest[21 : 21 + slots], rest[21 + slots :]
    held, held_down, rows_in, rows_grad, acts, sems = rest
    features = held.shape[0]
    width = held.shape[1] // 8
    half, quarter = features // 2, features // 4
    copies = [[] for _ in range(4)]
    first = pl.multiple_of(part_ref[0] * half, half)
    second = pl.multiple_of(half - part_ref[0] * half, half)
    count = 0
    for share, (group, lines) in enumerate(
        ((own, None), (near, None), (far, (first, second)), (far_near, (first, second)))
    ):
        for kind in range(3):
            target = held_down if kind == 2 else held
            column = share * width if kind == 2 else (2 * share + kind) * width
            columns = pl.ds(column, width)
            if share == 0:
                pairs = [(own[kind], target.at[:, columns])]
            elif share == 1:
                pairs = [(near.at[kind], target.at[:, columns])]
            else:
                pairs = [
                    (group[3 * side + kind], target.at[pl.ds(line, half), columns])
                    for side, line in enumerate(lines)
                ]
            for source, place in pairs:
                copies[share].append(pltpu.make_async_copy(source, place, sems.at[count]))
                count += 1
    for group in copies:
        for copy in group:
            copy.start()
    height = ins[0].shape[0]
    gates = []
    for slot, (in_ref, grad_ref) in enumerate(zip(ins, grads)):
        lines = slice(slot * height, (slot + 1) * height)
        rows_in[lines, :] = in_ref[...]
        rows_grad[lines, :] = grad_ref[:, :features]
        lanes = grad_ref[:, features:].astype(jnp.float32)
        gates.append(jnp.sum(lanes * lane_ref[...], axis=1, keepdims=True))
    gate = jnp.concatenate(gates)
    scaled_ref[...] = (gate * rows_grad[...].astype(jnp.float32)).astype(jnp.bfloat16)
    gate_sum = jnp.zeros(gate.shape, jnp.float32)
    for share in range(4):
        for copy in copies[share]:
            copy.wait()
        both = slice(2 * share * width, 2 * (share + 1) * width)
        pre = jnp.dot(rows_in[...], held[:, both], preferred_element_type=jnp.float32)
        pre_gate, pre_up = pre[:, :width], pre[:, width:]
        back_proj = jnp.dot(
            rows_grad[...],
            held_down[:, share * width : (share + 1) * width],
            preferred_element_type=jnp.float32,
        )
        sigmoid_g = jax.nn.sigmoid(pre_gate)
        activated = pre_gate * sigmoid_g
        hidden_act = activated * pre_up
        gate_sum = gate_sum + jnp.sum(back_proj * hidden_act, axis=1, keepdims=True)
        grad_hidden = gate * back_proj
        grad_gate = (
            grad_hidden * pre_up * sigmoid_g * (1.0 + pre_gate * (1.0 - sigmoid_g))
        ).astype(jnp.bfloat16)
        grad_up = (grad_hidden * activated).astype(jnp.bfloat16)
        acts[:, 2 * share * width : (2 * share + 1) * width] = grad_gate
        acts[:, (2 * share + 1) * width : 2 * (share + 1) * width] = grad_up
        hidden = hidden_send if share % 2 else hidden_keep
        pick = share // 2
        hidden[:, pick * width : (pick + 1) * width] = hidden_act.astype(jnp.bfloat16)
    near_ref[...] = acts[:, : 4 * width]
    far_ref[...] = acts[:, 4 * width :]
    for piece in range(4):
        lines = slice(piece * quarter, (piece + 1) * quarter)
        part = lax.dot_general(
            acts[...],
            held[lines, :],
            (((1,), (1,)), ((), ())),
            preferred_element_type=jnp.float32,
        ).astype(jnp.bfloat16)
        for slot, back in enumerate(backs):
            back[:, lines] = part[slot * height : (slot + 1) * height]
    for slot, back in enumerate(backs):
        back[:, features:] = jnp.broadcast_to(
            gate_sum[slot * height : (slot + 1) * height], (height, 128)
        ).astype(jnp.bfloat16)


def slot_compute(ins, grads, lane, part, weights):
    slots = len(ins)
    height = ins[0].shape[0]
    rows = slots * height
    features, width = weights[0].shape
    bf = jnp.bfloat16
    shapes = [(rows, c) for c in (4 * width, 4 * width, 2 * width, 2 * width, features)]
    shapes += [(height, features + 128)] * slots
    vmem = pl.BlockSpec(memory_space=pltpu.VMEM)
    out = pl.pallas_call(
        functools.partial(slot_kernel, slots),
        out_shape=[jax.ShapeDtypeStruct(shape, bf) for shape in shapes],
        in_specs=[vmem, pl.BlockSpec(memory_space=pltpu.SMEM)]
        + [vmem] * (2 * slots)
        + [pl.BlockSpec(memory_space=pl.ANY)] * 16,
        out_specs=[vmem] * len(shapes),
        scratch_shapes=[
            pltpu.VMEM((features, 8 * width), bf),
            pltpu.VMEM((features, 4 * width), bf),
            pltpu.VMEM((rows, features), bf),
            pltpu.VMEM((rows, features), bf),
            pltpu.VMEM((rows, 8 * width), bf),
            pltpu.SemaphoreType.DMA((18,)),
        ],
        compiler_params=pltpu.CompilerParams(vmem_limit_bytes=48 * 1024 * 1024),
        cost_estimate=pl.CostEstimate(
            flops=rows * features, bytes_accessed=2 * rows * features, transcendentals=0
        ),
    )(lane, part, *ins, *grads, *weights)
    return (*out[:5], out[5:])


def tied(*values):
    return lax.optimization_barrier(values)


def over_z(value, pairs):
    return lax.ppermute(value, "expert", pairs)


def over_x(value):
    return lax.ppermute(value, "replica", swap_x)


def over_core(value):
    return lax.ppermute(value, "replica", swap_core)


def over_parts(value):
    return lax.ppermute(value, "parts", swap_part)


def apart(step):
    return [(i, i ^ step) for i in range(4)]


def outer(lhs, rhs):
    return lax.dot_general(lhs, rhs, (((0,), (0,)), ((), ())), preferred_element_type=jnp.float32)


def fast_body(tokens, out_grad, expert_ids, gates, gate_weight, up_weight, down_weight):
    z = lax.axis_index("expert")
    y = lax.axis_index("parts")
    rows, features = tokens.shape
    bf, f32 = jnp.bfloat16, jnp.float32
    half = features // 2
    own = [gate_weight[0], up_weight[0], down_weight[0]]
    width = own[0].shape[1]
    halves = [lax.dynamic_slice_in_dim(w, y * half, half, 0) for w in own]
    lanes = jnp.arange(128, dtype=jnp.int32)[None, :]
    gate_lanes = sum(
        jnp.where(expert_ids[:, k : k + 1] == lanes, gates[:, k : k + 1], 0) for k in range(2)
    ).astype(bf)
    lane = (lanes == z).astype(f32)
    wide_grad = jnp.concatenate([out_grad, gate_lanes], axis=1)
    part_index = jnp.reshape(y, (1,)).astype(jnp.int32)

    in_two, in_one = over_z(tokens, apart(2)), over_z(tokens, apart(1))
    across = [over_x(w) for w in halves[:2]]
    other = [over_parts(across[0])]
    in_two, in_one, across[0], across[1], other[0], wide_grad, tokens_x, half_down, stacked = tied(
        in_two, in_one, *across, *other, wide_grad, tokens, halves[2], jnp.stack(own)
    )

    grad_two, grad_one = over_z(wide_grad, apart(2)), over_z(wide_grad, apart(1))
    across.append(over_x(half_down))
    other.append(over_parts(across[1]))
    near = over_core(stacked)
    across[2], near, tokens_x = tied(across[2], near, tokens_x)
    other.append(over_parts(across[2]))
    far_a = over_x(tokens_x)
    in_bc = jnp.concatenate([in_one, in_two])
    two = jnp.concatenate([in_two, grad_two], axis=1)
    two, grad_one, in_bc, far_a, *far_weights = tied(
        two, grad_one, in_bc, far_a, *across, *other
    )

    three = over_z(two, apart(1))
    far_bc = over_x(in_bc)
    weights = [*own, near, *far_weights, *[over_core(w) for w in far_weights]]
    acts_abc, crossing_abc, send_abc, keep_abc, scaled_abc, backs = slot_compute(
        [tokens, in_one, in_two], [wide_grad, grad_one, grad_two], lane, part_index, weights
    )
    three, far_bc, crossing_abc, back_a, back_b, back_c = tied(three, far_bc, crossing_abc, *backs)

    in_d, grad_d = three[:, :features], three[:, features:]
    cut = features * 11 // 16
    far_acts_abc = over_x(crossing_abc)
    back_two_low = over_z(back_c[:, :cut], apart(2))
    far_d = over_z(far_bc[rows:], apart(1))
    acts_d, crossing_d, send_d, keep_d, scaled_d, (back_d,) = slot_compute(
        [in_d], [grad_d], lane, part_index, weights
    )
    (far_acts_abc, back_two_low, far_d, acts_d, crossing_d, send_d, keep_d, scaled_d, back_d,
     back_b, back_c) = tied(
        far_acts_abc, back_two_low, far_d, acts_d, crossing_d, send_d, keep_d, scaled_d, back_d,
        back_b, back_c,
    )

    far_acts_d = over_x(crossing_d)
    back_two_high = over_z(back_c[:, cut:], apart(2))
    scaled = jnp.concatenate([scaled_abc, scaled_d])
    send = outer(scaled, jnp.concatenate([send_abc, send_d])).astype(bf)
    keep = outer(scaled, jnp.concatenate([keep_abc, keep_d])).astype(bf)
    both = keep.astype(f32) + over_core(send).astype(f32)
    crossing, both = both[:, width:].astype(bf), both[:, :width].astype(bf)
    far_acts_d, back_two_high, crossing, both, back_b, back_d = tied(
        far_acts_d, back_two_high, crossing, both, back_b, back_d
    )

    down_far = over_x(crossing)
    back_three = over_z(back_d, apart(3))
    back_one = over_z(back_b, apart(1))
    acts = jnp.concatenate([acts_abc, acts_d, far_acts_abc, far_acts_d])
    every_row = jnp.concatenate([tokens, in_bc, in_d, far_a, far_bc, far_d])
    send = over_core(outer(every_row, acts[:, 2 * width :]).astype(bf))
    pair = (outer(every_row, acts[:, : 2 * width]) + send.astype(f32)).astype(bf)
    gate_out, up_out = pair[:, :width], pair[:, width:]
    back_one, back_three, down_far, gate_out, up_out = tied(
        back_one, back_three, down_far, gate_out, up_out
    )
    back_two = jnp.concatenate([back_two_low, back_two_high], axis=1)
    returned = [back_a, back_one, back_two, back_three]
    down = (both.astype(f32) + down_far.astype(f32)).astype(bf)
    token_grad = sum(r[:, :features].astype(f32) for r in returned).astype(bf)
    gate_grad = sum(
        jnp.where(expert_ids == (z ^ step), r[:, features : features + 1].astype(f32), 0.0)
        for step, r in enumerate(returned)
    ).astype(bf)
    return token_grad, gate_grad, gate_out[None], up_out[None], down[None]


def body(*args):
    sizes = tuple(lax.axis_size(name) for name in ("parts", "expert", "replica"))
    if sizes == (2, 4, 4):
        return fast_body(*args)
    return general_body(*args)


def solution(mesh):
    in_specs = (
        P(("parts", "expert", "replica"), None),
        P(("parts", "expert", "replica"), None),
        P(("parts", "expert", "replica"), None),
        P(("parts", "expert", "replica"), None),
        P("expert", None, "replica"),
        P("expert", None, "replica"),
        P("expert", None, "replica"),
    )
    out_specs = (
        P(("parts", "expert", "replica"), None),
        P(("parts", "expert", "replica"), None),
        P(("parts", "expert"), None, "replica"),
        P(("parts", "expert"), None, "replica"),
        P(("parts", "expert"), None, "replica"),
    )
    return jax.shard_map(body, mesh=mesh, in_specs=in_specs, out_specs=out_specs, check_vma=False)
```

```python
import functools

import jax
import jax.numpy as jnp
from jax import lax
from jax.experimental import pallas as pl
from jax.experimental.pallas import tpu as pltpu
from jax.sharding import PartitionSpec as P

row_block = 256


def swiglu_backward(rows_in, rows_grad, rows_scaled, rows_gate, weight_g, weight_u, weight_d):
    pre_gate = jnp.dot(rows_in, weight_g, preferred_element_type=jnp.float32)
    pre_up = jnp.dot(rows_in, weight_u, preferred_element_type=jnp.float32)
    back_proj = jnp.dot(rows_grad, weight_d, preferred_element_type=jnp.float32)
    sigmoid_g = jax.nn.sigmoid(pre_gate)
    activated = pre_gate * sigmoid_g
    hidden_act = activated * pre_up
    gate_part = jnp.sum(back_proj * hidden_act, axis=1)
    grad_hidden = rows_gate[:, None] * back_proj
    grad_gate_pre = (
        grad_hidden * pre_up * sigmoid_g * (1.0 + pre_gate * (1.0 - sigmoid_g))
    ).astype(jnp.bfloat16)
    grad_up_pre = (grad_hidden * activated).astype(jnp.bfloat16)
    hidden_rounded = hidden_act.astype(jnp.bfloat16)
    contract_last = (((1,), (1,)), ((), ()))
    contract_first = (((0,), (0,)), ((), ()))
    input_grad = lax.dot_general(
        grad_gate_pre, weight_g, contract_last, preferred_element_type=jnp.float32
    )
    input_grad = input_grad + lax.dot_general(
        grad_up_pre, weight_u, contract_last, preferred_element_type=jnp.float32
    )
    add_gate = lax.dot_general(
        rows_in, grad_gate_pre, contract_first, preferred_element_type=jnp.float32
    )
    add_up = lax.dot_general(
        rows_in, grad_up_pre, contract_first, preferred_element_type=jnp.float32
    )
    add_down = lax.dot_general(
        rows_scaled, hidden_rounded, contract_first, preferred_element_type=jnp.float32
    )
    return (input_grad, gate_part, add_gate, add_up, add_down)


def hidden_part(state_now, pieces, first, row_data):
    gate_piece = pieces[0][0]
    up_piece = pieces[1][0]
    down_piece = pieces[2][0]
    rows_in, rows_grad, rows_scaled, rows_gate, block_total = row_data
    grad_g, grad_u, grad_d, input_acc, gate_acc = state_now
    packed = rows_in.shape[0]
    block_limit = packed // row_block

    def make_branch(block_count):
        row_total = block_count * row_block

        def branch(unused):
            input_grad, gate_part, add_g, add_u, add_d = swiglu_backward(
                rows_in[:row_total],
                rows_grad[:row_total],
                rows_scaled[:row_total],
                rows_gate[:row_total],
                gate_piece,
                up_piece,
                down_piece,
            )
            spare = packed - row_total
            input_grad = jnp.pad(input_grad, ((0, spare), (0, 0)))
            gate_part = jnp.pad(gate_part, ((0, spare),))
            return (input_grad, gate_part, add_g, add_u, add_d)

        return branch

    branches = [make_branch(count) for count in range(1, block_limit + 1)]
    which = jnp.clip(block_total - 1, 0, block_limit - 1)
    input_grad, gate_part, add_g, add_u, add_d = lax.switch(which, branches, 0)
    grad_g = lax.dynamic_update_slice_in_dim(grad_g, add_g, first, 1)
    grad_u = lax.dynamic_update_slice_in_dim(grad_u, add_u, first, 1)
    grad_d = lax.dynamic_update_slice_in_dim(grad_d, add_d, first, 1)
    return (grad_g, grad_u, grad_d, input_acc + input_grad, gate_acc + gate_part)


def general_body(tokens, out_grad, expert_ids, gates, gate_weight, up_weight, down_weight):
    tok_rows, feature_width = tokens.shape
    owners = lax.axis_size("expert")
    capacity = min(tok_rows, max(2, 6 * tok_rows // owners))
    slot_count = 2 * tok_rows
    flat_ids = expert_ids.reshape(-1)
    onehot = (flat_ids[:, None] == jnp.arange(owners, dtype=jnp.int32)[None, :]).astype(jnp.int32)
    before = jnp.cumsum(onehot, axis=0) - onehot
    position = jnp.sum(before * onehot, axis=1)
    target = flat_ids * capacity + position
    source = (
        jnp.full((owners * capacity,), slot_count, jnp.int32)
        .at[target]
        .set(jnp.arange(slot_count, dtype=jnp.int32))
    )
    in_ext = jnp.concatenate([tokens, jnp.zeros((1, feature_width), jnp.bfloat16)])
    grad_ext = jnp.concatenate([out_grad, jnp.zeros((1, feature_width), jnp.bfloat16)])
    gate_ext = jnp.concatenate([gates.reshape(-1), jnp.zeros((1,), jnp.bfloat16)])
    send_in = in_ext[source // 2].reshape(owners, capacity, feature_width)
    send_grad = grad_ext[source // 2].reshape(owners, capacity, feature_width)
    send_gate = gate_ext[source].reshape(owners, capacity)
    recv_in, recv_grad, recv_gate = (
        lax.all_to_all(send_in, "expert", split_axis=0, concat_axis=0, tiled=True),
        lax.all_to_all(send_grad, "expert", split_axis=0, concat_axis=0, tiled=True),
        lax.all_to_all(send_gate, "expert", split_axis=0, concat_axis=0, tiled=True),
    )
    recv_slots = owners * capacity
    live_rows = (recv_gate.reshape(-1) > 0).astype(jnp.int32)
    packed_pos = jnp.cumsum(live_rows) - live_rows
    live_total = jnp.sum(live_rows)
    packed = (recv_slots + row_block - 1) // row_block * row_block
    unpack = jnp.where(live_rows > 0, packed_pos, packed)
    pack_index = (
        jnp.full((packed,), recv_slots, jnp.int32)
        .at[unpack]
        .set(jnp.arange(recv_slots, dtype=jnp.int32), mode="drop")
    )
    rows_in = jnp.concatenate(
        [recv_in.reshape(recv_slots, feature_width), jnp.zeros((1, feature_width), jnp.bfloat16)]
    )[pack_index]
    rows_grad = jnp.concatenate(
        [recv_grad.reshape(recv_slots, feature_width), jnp.zeros((1, feature_width), jnp.bfloat16)]
    )[pack_index]
    rows_gate = jnp.concatenate([recv_gate.reshape(-1), jnp.zeros((1,), jnp.bfloat16)])[
        pack_index
    ].astype(jnp.float32)
    rows_scaled = (rows_gate[:, None] * rows_grad.astype(jnp.float32)).astype(jnp.bfloat16)
    block_total = (live_total + row_block - 1) // row_block
    row_data = (rows_in, rows_grad, rows_scaled, rows_gate, block_total)
    hidden_units = gate_weight.shape[2] * lax.axis_size("replica")
    zero_grad = jnp.zeros((feature_width, hidden_units), jnp.float32)
    start_state = (
        zero_grad,
        zero_grad,
        zero_grad,
        jnp.zeros((packed, feature_width), jnp.float32),
        jnp.zeros((packed,), jnp.float32),
    )
    complete = (
        lax.all_gather(gate_weight, "replica", axis=2, tiled=True),
        lax.all_gather(up_weight, "replica", axis=2, tiled=True),
        lax.all_gather(down_weight, "replica", axis=2, tiled=True),
    )
    final = hidden_part(start_state, complete, 0, row_data)
    grad_g, grad_u, grad_d, input_acc, gate_acc = final
    packed_grad = jnp.concatenate(
        [input_acc.astype(jnp.bfloat16), jnp.zeros((1, feature_width), jnp.bfloat16)]
    )
    packed_gate = jnp.concatenate([gate_acc.astype(jnp.bfloat16), jnp.zeros((1,), jnp.bfloat16)])
    back_grad = packed_grad[unpack].reshape(owners, capacity, feature_width)
    back_gate = packed_gate[unpack].reshape(owners, capacity)
    ret_grad, ret_gate = (
        lax.all_to_all(back_grad, "expert", split_axis=0, concat_axis=0, tiled=True),
        lax.all_to_all(back_gate, "expert", split_axis=0, concat_axis=0, tiled=True),
    )
    slot_grad = ret_grad.reshape(recv_slots, feature_width)[target].reshape(
        tok_rows, 2, feature_width
    )
    token_grad = slot_grad.astype(jnp.float32).sum(axis=1).astype(jnp.bfloat16)
    gate_grad = ret_gate.reshape(-1)[target].reshape(tok_rows, 2)
    shares = (
        lax.psum_scatter(
            grad_g.astype(jnp.bfloat16), "replica", scatter_dimension=1, tiled=True
        ).astype(jnp.float32),
        lax.psum_scatter(
            grad_u.astype(jnp.bfloat16), "replica", scatter_dimension=1, tiled=True
        ).astype(jnp.float32),
        lax.psum_scatter(
            grad_d.astype(jnp.bfloat16), "replica", scatter_dimension=1, tiled=True
        ).astype(jnp.float32),
    )
    return (
        token_grad,
        gate_grad,
        shares[0].astype(jnp.bfloat16)[None],
        shares[1].astype(jnp.bfloat16)[None],
        shares[2].astype(jnp.bfloat16)[None],
    )


swap_x = [(0, 2), (1, 3), (2, 0), (3, 1)]
swap_core = [(0, 1), (1, 0), (2, 3), (3, 2)]
swap_part = [(0, 1), (1, 0)]


def slot_kernel(slots, joined, later, cuts, splits, lane_ref, part_ref, *rest):
    count_in = slots * (1 if joined else 2)
    ins, rest = rest[:count_in], rest[count_in:]
    own, near, far, far_near = rest[:3], rest[3], rest[4:10], rest[10:16]
    rest = rest[16 + (4 if later else 0) :]
    kept, far_refs, rest = rest[:4], rest[4 : 4 + len(splits)], rest[4 + len(splits) :]
    backs, rest = rest[: len(cuts)], rest[len(cuts) :]
    held, held_down, rows_in, rows_grad, acts, sems = rest[:6]
    near_ref, hidden_send, hidden_keep, scaled_ref = rest[6:10] if later else kept
    _, features, width = held.shape
    half, eighth = features // 2, features // 8
    height = ins[0].shape[0]
    rows = slots * height
    copies = [[] for _ in range(4)]
    first = pl.multiple_of(part_ref[0] * half, half)
    second = pl.multiple_of(half - part_ref[0] * half, half)
    count = 0
    for share, (group, lines) in enumerate(
        ((own, None), (near, None), (far, (first, second)), (far_near, (first, second)))
    ):
        for kind in range(3):
            target = held_down.at[share] if kind == 2 else held.at[2 * share + kind]
            if share == 0:
                pairs = [(own[kind], target)]
            elif share == 1:
                pairs = [(near.at[kind], target)]
            else:
                pairs = [
                    (group[3 * side + kind], target.at[pl.ds(line, half), :])
                    for side, line in enumerate(lines)
                ]
            for source, place in pairs:
                copies[share].append(pltpu.make_async_copy(source, place, sems.at[count]))
                count += 1
    for group in copies:
        for copy in group:
            copy.start()
    gates = []
    for slot in range(slots):
        lines = slice(slot * height, (slot + 1) * height)
        grad_ref, begin = (ins[slot], features) if joined else (ins[slots + slot], 0)
        rows_in[lines, :] = ins[slot][:, :features]
        rows_grad[lines, :] = grad_ref[:, begin : begin + features]
        lanes = grad_ref[:, begin + features :].astype(jnp.float32)
        gates.append(jnp.sum(lanes * lane_ref[...], axis=1, keepdims=True))
    gate = jnp.concatenate(gates)
    scaled_ref[:rows, :] = (gate * rows_grad[...].astype(jnp.float32)).astype(jnp.bfloat16)
    gate_sum = jnp.zeros(gate.shape, jnp.float32)
    for share in range(4):
        for copy in copies[share]:
            copy.wait()
        pre_gate = jnp.dot(rows_in[...], held[2 * share], preferred_element_type=jnp.float32)
        pre_up = jnp.dot(rows_in[...], held[2 * share + 1], preferred_element_type=jnp.float32)
        back_proj = jnp.dot(rows_grad[...], held_down[share], preferred_element_type=jnp.float32)
        sigmoid_g = jax.nn.sigmoid(pre_gate)
        activated = pre_gate * sigmoid_g
        hidden_act = activated * pre_up
        gate_sum = gate_sum + jnp.sum(back_proj * hidden_act, axis=1, keepdims=True)
        grad_hidden = gate * back_proj
        grad_gate = (
            grad_hidden * pre_up * sigmoid_g * (1.0 + pre_gate * (1.0 - sigmoid_g))
        ).astype(jnp.bfloat16)
        grad_up = (grad_hidden * activated).astype(jnp.bfloat16)
        acts[:, 2 * share * width : (2 * share + 1) * width] = grad_gate
        acts[:, (2 * share + 1) * width : 2 * (share + 1) * width] = grad_up
        hidden = hidden_send if share % 2 else hidden_keep
        pick = share // 2
        hidden[:rows, pick * width : (pick + 1) * width] = hidden_act.astype(jnp.bfloat16)
    near_ref[:rows, :] = acts[:, : 4 * width]
    for far_ref, (begin, end) in zip(far_refs, splits):
        far_ref[...] = acts[begin:end, 4 * width :]
    stores = []
    if later:
        for place, source in enumerate((near_ref, hidden_send, hidden_keep, scaled_ref)):
            target = kept[place].at[pl.ds(kept[place].shape[0] - rows, rows), :]
            stores.append(pltpu.make_async_copy(source, target, sems.at[count + place]))
        for store in stores:
            store.start()
    for piece in range(8):
        lines = slice(piece * eighth, (piece + 1) * eighth)
        part = sum(
            lax.dot_general(
                acts[:, k * width : (k + 1) * width],
                held[k, lines, :],
                (((1,), (1,)), ((), ())),
                preferred_element_type=jnp.float32,
            )
            for k in range(8)
        ).astype(jnp.bfloat16)
        for back, (slot, begin, end) in zip(backs, cuts):
            if begin <= piece * eighth < end:
                back[:, piece * eighth - begin : (piece + 1) * eighth - begin] = part[
                    slot * height : (slot + 1) * height
                ]
    for back, (slot, begin, end) in zip(backs, cuts):
        if end > features:
            back[:, features - begin :] = jnp.broadcast_to(
                gate_sum[slot * height : (slot + 1) * height], (height, 128)
            ).astype(jnp.bfloat16)
    for store in stores:
        store.wait()


def slot_compute(ins, grads, lane, part, weights, total, cuts, splits, kept=()):
    slots = len(ins)
    height = ins[0].shape[0]
    rows = slots * height
    features, width = weights[0].shape
    bf = jnp.bfloat16
    columns = [4 * width, 2 * width, 2 * width, features]
    shapes = [(total, c) for c in columns] + [(end - begin, 4 * width) for begin, end in splits]
    shapes += [(height, end - begin) for _, begin, end in cuts]
    vmem = pl.BlockSpec(memory_space=pltpu.VMEM)
    anywhere = pl.BlockSpec(memory_space=pl.ANY)
    operands = [lane, part, *ins, *grads, *weights, *kept]
    out = pl.pallas_call(
        functools.partial(slot_kernel, slots, not grads, bool(kept), cuts, splits),
        out_shape=[jax.ShapeDtypeStruct(shape, bf) for shape in shapes],
        in_specs=[vmem, pl.BlockSpec(memory_space=pltpu.SMEM)]
        + [vmem] * (len(ins) + len(grads))
        + [anywhere] * (16 + len(kept)),
        out_specs=[anywhere if kept else vmem] * 4 + [vmem] * (len(shapes) - 4),
        scratch_shapes=[
            pltpu.VMEM((8, features, width), bf),
            pltpu.VMEM((4, features, width), bf),
            pltpu.VMEM((rows, features), bf),
            pltpu.VMEM((rows, features), bf),
            pltpu.VMEM((rows, 8 * width), bf),
            pltpu.SemaphoreType.DMA((22,)),
        ]
        + [pltpu.VMEM((rows, c), bf) for c in columns if kept],
        input_output_aliases={len(operands) - len(kept) + i: i for i in range(len(kept))},
        compiler_params=pltpu.CompilerParams(vmem_limit_bytes=48 * 1024 * 1024),
        cost_estimate=pl.CostEstimate(
            flops=rows * features, bytes_accessed=2 * rows * features, transcendentals=0
        ),
    )(*operands)
    return out[:4], out[4 : 4 + len(splits)], out[4 + len(splits) :]


def tied(*values):
    return lax.optimization_barrier(values)


def over_z(value, pairs):
    return lax.ppermute(value, "expert", pairs)


def over_x(value):
    return lax.ppermute(value, "replica", swap_x)


def over_core(value):
    return lax.ppermute(value, "replica", swap_core)


def over_parts(value):
    return lax.ppermute(value, "parts", swap_part)


def apart(step):
    return [(i, i ^ step) for i in range(4)]


def outer(lhs, rhs):
    return lax.dot_general(lhs, rhs, (((0,), (0,)), ((), ())), preferred_element_type=jnp.float32)


def fast_body(tokens, out_grad, expert_ids, gates, gate_weight, up_weight, down_weight):
    z = lax.axis_index("expert")
    y = lax.axis_index("parts")
    rows, features = tokens.shape
    bf, f32 = jnp.bfloat16, jnp.float32
    half = features // 2
    own = [gate_weight[0], up_weight[0], down_weight[0]]
    width = own[0].shape[1]
    halves = [lax.dynamic_slice_in_dim(w, y * half, half, 0) for w in own]
    lanes = jnp.arange(128, dtype=jnp.int32)[None, :]
    gate_lanes = sum(
        jnp.where(expert_ids[:, k : k + 1] == lanes, gates[:, k : k + 1], 0) for k in range(2)
    ).astype(bf)
    lane = (lanes == z).astype(f32)
    wide_grad = jnp.concatenate([out_grad, gate_lanes], axis=1)
    part_index = jnp.reshape(y, (1,)).astype(jnp.int32)

    in_two, in_one = over_z(tokens, apart(2)), over_z(tokens, apart(1))
    across = [over_x(w) for w in halves[:2]]
    other = [over_parts(across[0])]
    in_two, in_one, across[0], across[1], other[0], wide_grad, tokens_x, half_down, stacked = tied(
        in_two, in_one, *across, *other, wide_grad, tokens, halves[2], jnp.stack(own)
    )

    grad_two, grad_one = over_z(wide_grad, apart(2)), over_z(wide_grad, apart(1))
    across.append(over_x(half_down))
    other.append(over_parts(across[1]))
    near = over_core(stacked)
    across[2], near, tokens_x = tied(across[2], near, tokens_x)
    other.append(over_parts(across[2]))
    far_a = over_x(tokens_x)
    in_bc = jnp.concatenate([in_one, in_two])
    two = jnp.concatenate([in_two, grad_two], axis=1)
    two, grad_one, in_bc, far_a, *far_weights = tied(
        two, grad_one, in_bc, far_a, *across, *other
    )

    three = over_z(two, apart(1))
    far_bc = over_x(in_bc)
    weights = [*own, near, *far_weights, *[over_core(w) for w in far_weights]]
    slots, wide = 4, features + 128
    kept, (crossing_ab, crossing_c), backs = slot_compute(
        [tokens, in_one, in_two],
        [wide_grad, grad_one, grad_two],
        lane,
        part_index,
        weights,
        slots * rows,
        ((0, 0, wide), (1, 0, wide), (2, 0, half), (2, half, wide)),
        ((0, 2 * rows), (2 * rows, 3 * rows)),
    )
    three, far_bc, crossing_ab, crossing_c, *backs = tied(
        three, far_bc, crossing_ab, crossing_c, *backs
    )
    back_a, back_b, back_low, back_high = backs

    far_acts_ab = over_x(crossing_ab)
    back_two_low = over_z(back_low, apart(2))
    far_d_low = over_z(far_bc[rows:, :half], apart(1))
    kept, (crossing_d,), (back_d,) = slot_compute(
        [three], [], lane, part_index, weights, slots * rows, ((0, 0, wide),), ((0, rows),), kept
    )
    acts, hidden_send, hidden_keep, scaled = kept
    send = outer(scaled, hidden_send).astype(bf)
    crossing_cd = jnp.concatenate([crossing_c, crossing_d])
    far_acts_ab, back_two_low, far_d_low, crossing_cd, back_d, back_high, acts, send, scaled = tied(
        far_acts_ab, back_two_low, far_d_low, crossing_cd, back_d, back_high, acts, send, scaled
    )

    far_acts_cd = over_x(crossing_cd)
    back_two_high = over_z(back_high, apart(2))
    far_d_high = over_z(far_bc[rows:, half:], apart(1))
    keep = outer(scaled, hidden_keep).astype(bf)
    both = keep.astype(f32) + over_core(send).astype(f32)
    crossing, both = both[:, width:].astype(bf), both[:, :width].astype(bf)
    rows_first = jnp.concatenate([tokens, in_bc, three[:, :features], far_a, far_bc[:rows]])
    acts_first = jnp.concatenate([acts, far_acts_ab])
    first_keep = outer(rows_first, acts_first[:, : 2 * width]).astype(bf)
    far_acts_cd, back_two_high, far_d_high, crossing, both, back_d, back_b, first_keep = tied(
        far_acts_cd, back_two_high, far_d_high, crossing, both, back_d, back_b, first_keep
    )
    first_send = outer(rows_first, acts_first[:, 2 * width :]).astype(bf)

    down_far = over_x(crossing)
    back_three = over_z(back_d, apart(3))
    back_one = over_z(back_b, apart(1))
    back_two = jnp.concatenate([back_two_low, back_two_high], axis=1)
    rows_last = jnp.concatenate(
        [far_bc[rows:], jnp.concatenate([far_d_low, far_d_high], axis=1)]
    )
    send, keep = (
        outer(rows_last, far_acts_cd[:, cols]) + first.astype(f32)
        for cols, first in (
            (slice(2 * width, None), first_send),
            (slice(0, 2 * width), first_keep),
        )
    )
    send = send.astype(bf)
    got = over_core(send)
    pair = (keep + got.astype(f32)).astype(bf)
    gate_out, up_out = pair[:, :width], pair[:, width:]
    back_one, back_three, down_far, gate_out, up_out = tied(
        back_one, back_three, down_far, gate_out, up_out
    )
    returned = [back_a, back_one, back_two, back_three]
    down = (both.astype(f32) + down_far.astype(f32)).astype(bf)
    token_grad = sum(r[:, :features].astype(f32) for r in returned).astype(bf)
    gate_grad = sum(
        jnp.where(expert_ids == (z ^ step), r[:, features : features + 1].astype(f32), 0.0)
        for step, r in enumerate(returned)
    ).astype(bf)
    return token_grad, gate_grad, gate_out[None], up_out[None], down[None]


def body(*args):
    sizes = tuple(lax.axis_size(name) for name in ("parts", "expert", "replica"))
    if sizes == (2, 4, 4):
        return fast_body(*args)
    return general_body(*args)


def solution(mesh):
    in_specs = (
        P(("parts", "expert", "replica"), None),
        P(("parts", "expert", "replica"), None),
        P(("parts", "expert", "replica"), None),
        P(("parts", "expert", "replica"), None),
        P("expert", None, "replica"),
        P("expert", None, "replica"),
        P("expert", None, "replica"),
    )
    out_specs = (
        P(("parts", "expert", "replica"), None),
        P(("parts", "expert", "replica"), None),
        P(("parts", "expert"), None, "replica"),
        P(("parts", "expert"), None, "replica"),
        P(("parts", "expert"), None, "replica"),
    )
    return jax.shard_map(body, mesh=mesh, in_specs=in_specs, out_specs=out_specs, check_vma=False)
```

```python
import functools

import jax
import jax.numpy as jnp
from jax import lax
from jax.experimental import pallas as pl
from jax.experimental.pallas import tpu as pltpu
from jax.sharding import PartitionSpec as P

row_block = 256


def swiglu_backward(rows_in, rows_grad, rows_scaled, rows_gate, weight_g, weight_u, weight_d):
    pre_gate = jnp.dot(rows_in, weight_g, preferred_element_type=jnp.float32)
    pre_up = jnp.dot(rows_in, weight_u, preferred_element_type=jnp.float32)
    back_proj = jnp.dot(rows_grad, weight_d, preferred_element_type=jnp.float32)
    sigmoid_g = jax.nn.sigmoid(pre_gate)
    activated = pre_gate * sigmoid_g
    hidden_act = activated * pre_up
    gate_part = jnp.sum(back_proj * hidden_act, axis=1)
    grad_hidden = rows_gate[:, None] * back_proj
    grad_gate_pre = (
        grad_hidden * pre_up * sigmoid_g * (1.0 + pre_gate * (1.0 - sigmoid_g))
    ).astype(jnp.bfloat16)
    grad_up_pre = (grad_hidden * activated).astype(jnp.bfloat16)
    hidden_rounded = hidden_act.astype(jnp.bfloat16)
    contract_last = (((1,), (1,)), ((), ()))
    contract_first = (((0,), (0,)), ((), ()))
    input_grad = lax.dot_general(
        grad_gate_pre, weight_g, contract_last, preferred_element_type=jnp.float32
    )
    input_grad = input_grad + lax.dot_general(
        grad_up_pre, weight_u, contract_last, preferred_element_type=jnp.float32
    )
    add_gate = lax.dot_general(
        rows_in, grad_gate_pre, contract_first, preferred_element_type=jnp.float32
    )
    add_up = lax.dot_general(
        rows_in, grad_up_pre, contract_first, preferred_element_type=jnp.float32
    )
    add_down = lax.dot_general(
        rows_scaled, hidden_rounded, contract_first, preferred_element_type=jnp.float32
    )
    return (input_grad, gate_part, add_gate, add_up, add_down)


def hidden_part(state_now, pieces, first, row_data):
    gate_piece = pieces[0][0]
    up_piece = pieces[1][0]
    down_piece = pieces[2][0]
    rows_in, rows_grad, rows_scaled, rows_gate, block_total = row_data
    grad_g, grad_u, grad_d, input_acc, gate_acc = state_now
    packed = rows_in.shape[0]
    block_limit = packed // row_block

    def make_branch(block_count):
        row_total = block_count * row_block

        def branch(unused):
            input_grad, gate_part, add_g, add_u, add_d = swiglu_backward(
                rows_in[:row_total],
                rows_grad[:row_total],
                rows_scaled[:row_total],
                rows_gate[:row_total],
                gate_piece,
                up_piece,
                down_piece,
            )
            spare = packed - row_total
            input_grad = jnp.pad(input_grad, ((0, spare), (0, 0)))
            gate_part = jnp.pad(gate_part, ((0, spare),))
            return (input_grad, gate_part, add_g, add_u, add_d)

        return branch

    branches = [make_branch(count) for count in range(1, block_limit + 1)]
    which = jnp.clip(block_total - 1, 0, block_limit - 1)
    input_grad, gate_part, add_g, add_u, add_d = lax.switch(which, branches, 0)
    grad_g = lax.dynamic_update_slice_in_dim(grad_g, add_g, first, 1)
    grad_u = lax.dynamic_update_slice_in_dim(grad_u, add_u, first, 1)
    grad_d = lax.dynamic_update_slice_in_dim(grad_d, add_d, first, 1)
    return (grad_g, grad_u, grad_d, input_acc + input_grad, gate_acc + gate_part)


def general_body(tokens, out_grad, expert_ids, gates, gate_weight, up_weight, down_weight):
    tok_rows, feature_width = tokens.shape
    owners = lax.axis_size("expert")
    capacity = min(tok_rows, max(2, 6 * tok_rows // owners))
    slot_count = 2 * tok_rows
    flat_ids = expert_ids.reshape(-1)
    onehot = (flat_ids[:, None] == jnp.arange(owners, dtype=jnp.int32)[None, :]).astype(jnp.int32)
    before = jnp.cumsum(onehot, axis=0) - onehot
    position = jnp.sum(before * onehot, axis=1)
    target = flat_ids * capacity + position
    source = (
        jnp.full((owners * capacity,), slot_count, jnp.int32)
        .at[target]
        .set(jnp.arange(slot_count, dtype=jnp.int32))
    )
    in_ext = jnp.concatenate([tokens, jnp.zeros((1, feature_width), jnp.bfloat16)])
    grad_ext = jnp.concatenate([out_grad, jnp.zeros((1, feature_width), jnp.bfloat16)])
    gate_ext = jnp.concatenate([gates.reshape(-1), jnp.zeros((1,), jnp.bfloat16)])
    send_in = in_ext[source // 2].reshape(owners, capacity, feature_width)
    send_grad = grad_ext[source // 2].reshape(owners, capacity, feature_width)
    send_gate = gate_ext[source].reshape(owners, capacity)
    recv_in, recv_grad, recv_gate = (
        lax.all_to_all(send_in, "expert", split_axis=0, concat_axis=0, tiled=True),
        lax.all_to_all(send_grad, "expert", split_axis=0, concat_axis=0, tiled=True),
        lax.all_to_all(send_gate, "expert", split_axis=0, concat_axis=0, tiled=True),
    )
    recv_slots = owners * capacity
    live_rows = (recv_gate.reshape(-1) > 0).astype(jnp.int32)
    packed_pos = jnp.cumsum(live_rows) - live_rows
    live_total = jnp.sum(live_rows)
    packed = (recv_slots + row_block - 1) // row_block * row_block
    unpack = jnp.where(live_rows > 0, packed_pos, packed)
    pack_index = (
        jnp.full((packed,), recv_slots, jnp.int32)
        .at[unpack]
        .set(jnp.arange(recv_slots, dtype=jnp.int32), mode="drop")
    )
    rows_in = jnp.concatenate(
        [recv_in.reshape(recv_slots, feature_width), jnp.zeros((1, feature_width), jnp.bfloat16)]
    )[pack_index]
    rows_grad = jnp.concatenate(
        [recv_grad.reshape(recv_slots, feature_width), jnp.zeros((1, feature_width), jnp.bfloat16)]
    )[pack_index]
    rows_gate = jnp.concatenate([recv_gate.reshape(-1), jnp.zeros((1,), jnp.bfloat16)])[
        pack_index
    ].astype(jnp.float32)
    rows_scaled = (rows_gate[:, None] * rows_grad.astype(jnp.float32)).astype(jnp.bfloat16)
    block_total = (live_total + row_block - 1) // row_block
    row_data = (rows_in, rows_grad, rows_scaled, rows_gate, block_total)
    hidden_units = gate_weight.shape[2] * lax.axis_size("replica")
    zero_grad = jnp.zeros((feature_width, hidden_units), jnp.float32)
    start_state = (
        zero_grad,
        zero_grad,
        zero_grad,
        jnp.zeros((packed, feature_width), jnp.float32),
        jnp.zeros((packed,), jnp.float32),
    )
    complete = (
        lax.all_gather(gate_weight, "replica", axis=2, tiled=True),
        lax.all_gather(up_weight, "replica", axis=2, tiled=True),
        lax.all_gather(down_weight, "replica", axis=2, tiled=True),
    )
    final = hidden_part(start_state, complete, 0, row_data)
    grad_g, grad_u, grad_d, input_acc, gate_acc = final
    packed_grad = jnp.concatenate(
        [input_acc.astype(jnp.bfloat16), jnp.zeros((1, feature_width), jnp.bfloat16)]
    )
    packed_gate = jnp.concatenate([gate_acc.astype(jnp.bfloat16), jnp.zeros((1,), jnp.bfloat16)])
    back_grad = packed_grad[unpack].reshape(owners, capacity, feature_width)
    back_gate = packed_gate[unpack].reshape(owners, capacity)
    ret_grad, ret_gate = (
        lax.all_to_all(back_grad, "expert", split_axis=0, concat_axis=0, tiled=True),
        lax.all_to_all(back_gate, "expert", split_axis=0, concat_axis=0, tiled=True),
    )
    slot_grad = ret_grad.reshape(recv_slots, feature_width)[target].reshape(
        tok_rows, 2, feature_width
    )
    token_grad = slot_grad.astype(jnp.float32).sum(axis=1).astype(jnp.bfloat16)
    gate_grad = ret_gate.reshape(-1)[target].reshape(tok_rows, 2)
    shares = (
        lax.psum_scatter(
            grad_g.astype(jnp.bfloat16), "replica", scatter_dimension=1, tiled=True
        ).astype(jnp.float32),
        lax.psum_scatter(
            grad_u.astype(jnp.bfloat16), "replica", scatter_dimension=1, tiled=True
        ).astype(jnp.float32),
        lax.psum_scatter(
            grad_d.astype(jnp.bfloat16), "replica", scatter_dimension=1, tiled=True
        ).astype(jnp.float32),
    )
    return (
        token_grad,
        gate_grad,
        shares[0].astype(jnp.bfloat16)[None],
        shares[1].astype(jnp.bfloat16)[None],
        shares[2].astype(jnp.bfloat16)[None],
    )


swap_x = [(0, 2), (1, 3), (2, 0), (3, 1)]
swap_core = [(0, 1), (1, 0), (2, 3), (3, 2)]
swap_part = [(0, 1), (1, 0)]


def slot_kernel(slots, joined, later, cuts, splits, lane_ref, part_ref, *rest):
    count_in = slots * (1 if joined else 2)
    ins, rest = rest[:count_in], rest[count_in:]
    own, near, far, far_near = rest[:3], rest[3], rest[4:10], rest[10:16]
    rest = rest[16 + (4 if later else 0) :]
    kept, far_refs, rest = rest[:4], rest[4 : 4 + len(splits)], rest[4 + len(splits) :]
    backs, rest = rest[: len(cuts)], rest[len(cuts) :]
    held, held_down, rows_in, rows_grad, acts, sems = rest[:6]
    near_ref, hidden_send, hidden_keep, scaled_ref = rest[6:10] if later else kept
    _, features, width = held.shape
    half, eighth = features // 2, features // 8
    height = ins[0].shape[0]
    rows = slots * height
    copies = [[] for _ in range(4)]
    first = pl.multiple_of(part_ref[0] * half, half)
    second = pl.multiple_of(half - part_ref[0] * half, half)
    count = 0
    for share, (group, lines) in enumerate(
        ((own, None), (near, None), (far, (first, second)), (far_near, (first, second)))
    ):
        for kind in range(3):
            target = held_down.at[share] if kind == 2 else held.at[2 * share + kind]
            if share == 0:
                pairs = [(own[kind], target)]
            elif share == 1:
                pairs = [(near.at[kind], target)]
            else:
                pairs = [
                    (group[3 * side + kind], target.at[pl.ds(line, half), :])
                    for side, line in enumerate(lines)
                ]
            for source, place in pairs:
                copies[share].append(pltpu.make_async_copy(source, place, sems.at[count]))
                count += 1
    for group in copies:
        for copy in group:
            copy.start()
    gates = []
    for slot in range(slots):
        lines = slice(slot * height, (slot + 1) * height)
        grad_ref, begin = (ins[slot], features) if joined else (ins[slots + slot], 0)
        rows_in[lines, :] = ins[slot][:, :features]
        rows_grad[lines, :] = grad_ref[:, begin : begin + features]
        lanes = grad_ref[:, begin + features :].astype(jnp.float32)
        gates.append(jnp.sum(lanes * lane_ref[...], axis=1, keepdims=True))
    gate = jnp.concatenate(gates)
    scaled_ref[:rows, :] = (gate * rows_grad[...].astype(jnp.float32)).astype(jnp.bfloat16)
    gate_sum = jnp.zeros(gate.shape, jnp.float32)
    for share in range(4):
        for copy in copies[share]:
            copy.wait()
        pre_gate = jnp.dot(rows_in[...], held[2 * share], preferred_element_type=jnp.float32)
        pre_up = jnp.dot(rows_in[...], held[2 * share + 1], preferred_element_type=jnp.float32)
        back_proj = jnp.dot(rows_grad[...], held_down[share], preferred_element_type=jnp.float32)
        sigmoid_g = jax.nn.sigmoid(pre_gate)
        activated = pre_gate * sigmoid_g
        hidden_act = activated * pre_up
        gate_sum = gate_sum + jnp.sum(back_proj * hidden_act, axis=1, keepdims=True)
        grad_hidden = gate * back_proj
        grad_gate = (
            grad_hidden * pre_up * sigmoid_g * (1.0 + pre_gate * (1.0 - sigmoid_g))
        ).astype(jnp.bfloat16)
        grad_up = (grad_hidden * activated).astype(jnp.bfloat16)
        acts[:, 2 * share * width : (2 * share + 1) * width] = grad_gate
        acts[:, (2 * share + 1) * width : 2 * (share + 1) * width] = grad_up
        hidden = hidden_send if share % 2 else hidden_keep
        pick = share // 2
        hidden[:rows, pick * width : (pick + 1) * width] = hidden_act.astype(jnp.bfloat16)
    near_ref[:rows, :] = acts[:, : 4 * width]
    for far_ref, (begin, end) in zip(far_refs, splits):
        far_ref[...] = acts[begin:end, 4 * width :]
    stores = []
    if later:
        for place, source in enumerate((near_ref, hidden_send, hidden_keep, scaled_ref)):
            target = kept[place].at[pl.ds(kept[place].shape[0] - rows, rows), :]
            stores.append(pltpu.make_async_copy(source, target, sems.at[count + place]))
        for store in stores:
            store.start()
    for piece in range(8):
        lines = slice(piece * eighth, (piece + 1) * eighth)
        part = sum(
            lax.dot_general(
                acts[:, k * width : (k + 1) * width],
                held[k, lines, :],
                (((1,), (1,)), ((), ())),
                preferred_element_type=jnp.float32,
            )
            for k in range(8)
        ).astype(jnp.bfloat16)
        for back, (slot, begin, end) in zip(backs, cuts):
            if begin <= piece * eighth < end:
                back[:, piece * eighth - begin : (piece + 1) * eighth - begin] = part[
                    slot * height : (slot + 1) * height
                ]
    for back, (slot, begin, end) in zip(backs, cuts):
        if end > features:
            back[:, features - begin :] = jnp.broadcast_to(
                gate_sum[slot * height : (slot + 1) * height], (height, 128)
            ).astype(jnp.bfloat16)
    for store in stores:
        store.wait()


def slot_compute(ins, grads, lane, part, weights, total, cuts, splits, kept=()):
    slots = len(ins)
    height = ins[0].shape[0]
    rows = slots * height
    features, width = weights[0].shape
    bf = jnp.bfloat16
    columns = [4 * width, 2 * width, 2 * width, features]
    shapes = [(total, c) for c in columns] + [(end - begin, 4 * width) for begin, end in splits]
    shapes += [(height, end - begin) for _, begin, end in cuts]
    vmem = pl.BlockSpec(memory_space=pltpu.VMEM)
    anywhere = pl.BlockSpec(memory_space=pl.ANY)
    operands = [lane, part, *ins, *grads, *weights, *kept]
    out = pl.pallas_call(
        functools.partial(slot_kernel, slots, not grads, bool(kept), cuts, splits),
        out_shape=[jax.ShapeDtypeStruct(shape, bf) for shape in shapes],
        in_specs=[vmem, pl.BlockSpec(memory_space=pltpu.SMEM)]
        + [vmem] * (len(ins) + len(grads))
        + [anywhere] * (16 + len(kept)),
        out_specs=[anywhere if kept else vmem] * 4 + [vmem] * (len(shapes) - 4),
        scratch_shapes=[
            pltpu.VMEM((8, features, width), bf),
            pltpu.VMEM((4, features, width), bf),
            pltpu.VMEM((rows, features), bf),
            pltpu.VMEM((rows, features), bf),
            pltpu.VMEM((rows, 8 * width), bf),
            pltpu.SemaphoreType.DMA((22,)),
        ]
        + [pltpu.VMEM((rows, c), bf) for c in columns if kept],
        input_output_aliases={len(operands) - len(kept) + i: i for i in range(len(kept))},
        compiler_params=pltpu.CompilerParams(vmem_limit_bytes=48 * 1024 * 1024),
        cost_estimate=pl.CostEstimate(
            flops=rows * features, bytes_accessed=2 * rows * features, transcendentals=0
        ),
    )(*operands)
    return out[:4], out[4 : 4 + len(splits)], out[4 + len(splits) :]


def tied(*values):
    return lax.optimization_barrier(values)


def over_z(value, pairs):
    return lax.ppermute(value, "expert", pairs)


def over_x(value):
    return lax.ppermute(value, "replica", swap_x)


def over_core(value):
    return lax.ppermute(value, "replica", swap_core)


def over_parts(value):
    return lax.ppermute(value, "parts", swap_part)


def apart(step):
    return [(i, i ^ step) for i in range(4)]


def outer(lhs, rhs):
    return lax.dot_general(lhs, rhs, (((0,), (0,)), ((), ())), preferred_element_type=jnp.float32)


def fast_body(tokens, out_grad, expert_ids, gates, gate_weight, up_weight, down_weight):
    z = lax.axis_index("expert")
    y = lax.axis_index("parts")
    rows, features = tokens.shape
    bf, f32 = jnp.bfloat16, jnp.float32
    half = features // 2
    own = [gate_weight[0], up_weight[0], down_weight[0]]
    width = own[0].shape[1]
    halves = [lax.dynamic_slice_in_dim(w, y * half, half, 0) for w in own]
    lanes = jnp.arange(128, dtype=jnp.int32)[None, :]
    gate_lanes = sum(
        jnp.where(expert_ids[:, k : k + 1] == lanes, gates[:, k : k + 1], 0) for k in range(2)
    ).astype(bf)
    lane = (lanes == z).astype(f32)
    wide_grad = jnp.concatenate([out_grad, gate_lanes], axis=1)
    part_index = jnp.reshape(y, (1,)).astype(jnp.int32)

    in_two, in_one = over_z(tokens, apart(2)), over_z(tokens, apart(1))
    across = [over_x(w) for w in halves[:2]]
    other = [over_parts(across[0])]
    in_two, in_one, across[0], across[1], other[0], wide_grad, tokens_x, half_down, stacked = tied(
        in_two, in_one, *across, *other, wide_grad, tokens, halves[2], jnp.stack(own)
    )

    grad_two, grad_one = over_z(wide_grad, apart(2)), over_z(wide_grad, apart(1))
    across.append(over_x(half_down))
    other.append(over_parts(across[1]))
    near = over_core(stacked)
    across[2], near, tokens_x = tied(across[2], near, tokens_x)
    other.append(over_parts(across[2]))
    far_a = over_x(tokens_x)
    in_bc = jnp.concatenate([in_one, in_two])
    two = jnp.concatenate([in_two, grad_two], axis=1)
    two, grad_one, in_bc, far_a, *far_weights = tied(
        two, grad_one, in_bc, far_a, *across, *other
    )

    three = over_z(two, apart(1))
    far_bc = over_x(in_bc)
    weights = [*own, near, *far_weights, *[over_core(w) for w in far_weights]]
    slots, wide, cut = 4, features + 128, features * 5 // 8
    kept, (crossing_abc,), backs = slot_compute(
        [tokens, in_one, in_two],
        [wide_grad, grad_one, grad_two],
        lane,
        part_index,
        weights,
        slots * rows,
        ((0, 0, wide), (1, 0, wide), (2, 0, cut), (2, cut, wide)),
        ((0, 3 * rows),),
    )
    three, far_bc, crossing_abc, *backs = tied(three, far_bc, crossing_abc, *backs)
    back_a, back_b, back_low, back_high = backs

    far_acts_abc = over_x(crossing_abc)
    back_two_low = over_z(back_low, apart(2))
    far_d_low = over_z(far_bc[rows:, :half], apart(1))
    kept, (crossing_d,), (back_d,) = slot_compute(
        [three], [], lane, part_index, weights, slots * rows, ((0, 0, wide),), ((0, rows),), kept
    )
    acts, hidden_send, hidden_keep, scaled = kept
    send = outer(scaled, hidden_send).astype(bf)
    far_acts_abc, back_two_low, far_d_low, crossing_d, back_d, back_high, acts, send, scaled = tied(
        far_acts_abc, back_two_low, far_d_low, crossing_d, back_d, back_high, acts, send, scaled
    )

    far_acts_d = over_x(crossing_d)
    back_two_high = over_z(back_high, apart(2))
    far_d_high = over_z(far_bc[rows:, half:], apart(1))
    keep = outer(scaled, hidden_keep).astype(bf)
    both = keep.astype(f32) + over_core(send).astype(f32)
    crossing, both = both[:, width:].astype(bf), both[:, :width].astype(bf)
    rows_first = jnp.concatenate([tokens, in_bc, three[:, :features], far_a, far_bc[:rows]])
    acts_first = jnp.concatenate([acts, far_acts_abc[: 2 * rows]])
    first_keep = outer(rows_first, acts_first[:, : 2 * width]).astype(bf)
    far_acts_d, back_two_high, far_d_high, crossing, both, back_d, back_b, first_keep = tied(
        far_acts_d, back_two_high, far_d_high, crossing, both, back_d, back_b, first_keep
    )
    first_send = outer(rows_first, acts_first[:, 2 * width :]).astype(bf)

    down_far = over_x(crossing)
    back_three = over_z(back_d, apart(3))
    back_one = over_z(back_b, apart(1))
    back_two = jnp.concatenate([back_two_low, back_two_high], axis=1)
    rows_last = jnp.concatenate(
        [far_bc[rows:], jnp.concatenate([far_d_low, far_d_high], axis=1)]
    )
    acts_last = jnp.concatenate([far_acts_abc[2 * rows :], far_acts_d])
    send, keep = (
        outer(rows_last, acts_last[:, cols]) + first.astype(f32)
        for cols, first in (
            (slice(2 * width, None), first_send),
            (slice(0, 2 * width), first_keep),
        )
    )
    send = send.astype(bf)
    got = over_core(send)
    pair = (keep + got.astype(f32)).astype(bf)
    gate_out, up_out = pair[:, :width], pair[:, width:]
    back_one, back_three, down_far, gate_out, up_out = tied(
        back_one, back_three, down_far, gate_out, up_out
    )
    returned = [back_a, back_one, back_two, back_three]
    down = (both.astype(f32) + down_far.astype(f32)).astype(bf)
    token_grad = sum(r[:, :features].astype(f32) for r in returned).astype(bf)
    gate_grad = sum(
        jnp.where(expert_ids == (z ^ step), r[:, features : features + 1].astype(f32), 0.0)
        for step, r in enumerate(returned)
    ).astype(bf)
    return token_grad, gate_grad, gate_out[None], up_out[None], down[None]


def body(*args):
    sizes = tuple(lax.axis_size(name) for name in ("parts", "expert", "replica"))
    if sizes == (2, 4, 4):
        return fast_body(*args)
    return general_body(*args)


def solution(mesh):
    in_specs = (
        P(("parts", "expert", "replica"), None),
        P(("parts", "expert", "replica"), None),
        P(("parts", "expert", "replica"), None),
        P(("parts", "expert", "replica"), None),
        P("expert", None, "replica"),
        P("expert", None, "replica"),
        P("expert", None, "replica"),
    )
    out_specs = (
        P(("parts", "expert", "replica"), None),
        P(("parts", "expert", "replica"), None),
        P(("parts", "expert"), None, "replica"),
        P(("parts", "expert"), None, "replica"),
        P(("parts", "expert"), None, "replica"),
    )
    return jax.shard_map(body, mesh=mesh, in_specs=in_specs, out_specs=out_specs, check_vma=False)
```

```python
import functools

import jax
import jax.numpy as jnp
from jax import lax
from jax.experimental import pallas as pl
from jax.experimental.pallas import tpu as pltpu
from jax.sharding import PartitionSpec as P

row_block = 256


def swiglu_backward(rows_in, rows_grad, rows_scaled, rows_gate, weight_g, weight_u, weight_d):
    pre_gate = jnp.dot(rows_in, weight_g, preferred_element_type=jnp.float32)
    pre_up = jnp.dot(rows_in, weight_u, preferred_element_type=jnp.float32)
    back_proj = jnp.dot(rows_grad, weight_d, preferred_element_type=jnp.float32)
    sigmoid_g = jax.nn.sigmoid(pre_gate)
    activated = pre_gate * sigmoid_g
    hidden_act = activated * pre_up
    gate_part = jnp.sum(back_proj * hidden_act, axis=1)
    grad_hidden = rows_gate[:, None] * back_proj
    grad_gate_pre = (
        grad_hidden * pre_up * sigmoid_g * (1.0 + pre_gate * (1.0 - sigmoid_g))
    ).astype(jnp.bfloat16)
    grad_up_pre = (grad_hidden * activated).astype(jnp.bfloat16)
    hidden_rounded = hidden_act.astype(jnp.bfloat16)
    contract_last = (((1,), (1,)), ((), ()))
    contract_first = (((0,), (0,)), ((), ()))
    input_grad = lax.dot_general(
        grad_gate_pre, weight_g, contract_last, preferred_element_type=jnp.float32
    )
    input_grad = input_grad + lax.dot_general(
        grad_up_pre, weight_u, contract_last, preferred_element_type=jnp.float32
    )
    add_gate = lax.dot_general(
        rows_in, grad_gate_pre, contract_first, preferred_element_type=jnp.float32
    )
    add_up = lax.dot_general(
        rows_in, grad_up_pre, contract_first, preferred_element_type=jnp.float32
    )
    add_down = lax.dot_general(
        rows_scaled, hidden_rounded, contract_first, preferred_element_type=jnp.float32
    )
    return (input_grad, gate_part, add_gate, add_up, add_down)


def hidden_part(state_now, pieces, first, row_data):
    gate_piece = pieces[0][0]
    up_piece = pieces[1][0]
    down_piece = pieces[2][0]
    rows_in, rows_grad, rows_scaled, rows_gate, block_total = row_data
    grad_g, grad_u, grad_d, input_acc, gate_acc = state_now
    packed = rows_in.shape[0]
    block_limit = packed // row_block

    def make_branch(block_count):
        row_total = block_count * row_block

        def branch(unused):
            input_grad, gate_part, add_g, add_u, add_d = swiglu_backward(
                rows_in[:row_total],
                rows_grad[:row_total],
                rows_scaled[:row_total],
                rows_gate[:row_total],
                gate_piece,
                up_piece,
                down_piece,
            )
            spare = packed - row_total
            input_grad = jnp.pad(input_grad, ((0, spare), (0, 0)))
            gate_part = jnp.pad(gate_part, ((0, spare),))
            return (input_grad, gate_part, add_g, add_u, add_d)

        return branch

    branches = [make_branch(count) for count in range(1, block_limit + 1)]
    which = jnp.clip(block_total - 1, 0, block_limit - 1)
    input_grad, gate_part, add_g, add_u, add_d = lax.switch(which, branches, 0)
    grad_g = lax.dynamic_update_slice_in_dim(grad_g, add_g, first, 1)
    grad_u = lax.dynamic_update_slice_in_dim(grad_u, add_u, first, 1)
    grad_d = lax.dynamic_update_slice_in_dim(grad_d, add_d, first, 1)
    return (grad_g, grad_u, grad_d, input_acc + input_grad, gate_acc + gate_part)


def general_body(tokens, out_grad, expert_ids, gates, gate_weight, up_weight, down_weight):
    tok_rows, feature_width = tokens.shape
    owners = lax.axis_size("expert")
    capacity = min(tok_rows, max(2, 6 * tok_rows // owners))
    slot_count = 2 * tok_rows
    flat_ids = expert_ids.reshape(-1)
    onehot = (flat_ids[:, None] == jnp.arange(owners, dtype=jnp.int32)[None, :]).astype(jnp.int32)
    before = jnp.cumsum(onehot, axis=0) - onehot
    position = jnp.sum(before * onehot, axis=1)
    target = flat_ids * capacity + position
    source = (
        jnp.full((owners * capacity,), slot_count, jnp.int32)
        .at[target]
        .set(jnp.arange(slot_count, dtype=jnp.int32))
    )
    in_ext = jnp.concatenate([tokens, jnp.zeros((1, feature_width), jnp.bfloat16)])
    grad_ext = jnp.concatenate([out_grad, jnp.zeros((1, feature_width), jnp.bfloat16)])
    gate_ext = jnp.concatenate([gates.reshape(-1), jnp.zeros((1,), jnp.bfloat16)])
    send_in = in_ext[source // 2].reshape(owners, capacity, feature_width)
    send_grad = grad_ext[source // 2].reshape(owners, capacity, feature_width)
    send_gate = gate_ext[source].reshape(owners, capacity)
    recv_in, recv_grad, recv_gate = (
        lax.all_to_all(send_in, "expert", split_axis=0, concat_axis=0, tiled=True),
        lax.all_to_all(send_grad, "expert", split_axis=0, concat_axis=0, tiled=True),
        lax.all_to_all(send_gate, "expert", split_axis=0, concat_axis=0, tiled=True),
    )
    recv_slots = owners * capacity
    live_rows = (recv_gate.reshape(-1) > 0).astype(jnp.int32)
    packed_pos = jnp.cumsum(live_rows) - live_rows
    live_total = jnp.sum(live_rows)
    packed = (recv_slots + row_block - 1) // row_block * row_block
    unpack = jnp.where(live_rows > 0, packed_pos, packed)
    pack_index = (
        jnp.full((packed,), recv_slots, jnp.int32)
        .at[unpack]
        .set(jnp.arange(recv_slots, dtype=jnp.int32), mode="drop")
    )
    rows_in = jnp.concatenate(
        [recv_in.reshape(recv_slots, feature_width), jnp.zeros((1, feature_width), jnp.bfloat16)]
    )[pack_index]
    rows_grad = jnp.concatenate(
        [recv_grad.reshape(recv_slots, feature_width), jnp.zeros((1, feature_width), jnp.bfloat16)]
    )[pack_index]
    rows_gate = jnp.concatenate([recv_gate.reshape(-1), jnp.zeros((1,), jnp.bfloat16)])[
        pack_index
    ].astype(jnp.float32)
    rows_scaled = (rows_gate[:, None] * rows_grad.astype(jnp.float32)).astype(jnp.bfloat16)
    block_total = (live_total + row_block - 1) // row_block
    row_data = (rows_in, rows_grad, rows_scaled, rows_gate, block_total)
    hidden_units = gate_weight.shape[2] * lax.axis_size("replica")
    zero_grad = jnp.zeros((feature_width, hidden_units), jnp.float32)
    start_state = (
        zero_grad,
        zero_grad,
        zero_grad,
        jnp.zeros((packed, feature_width), jnp.float32),
        jnp.zeros((packed,), jnp.float32),
    )
    complete = (
        lax.all_gather(gate_weight, "replica", axis=2, tiled=True),
        lax.all_gather(up_weight, "replica", axis=2, tiled=True),
        lax.all_gather(down_weight, "replica", axis=2, tiled=True),
    )
    final = hidden_part(start_state, complete, 0, row_data)
    grad_g, grad_u, grad_d, input_acc, gate_acc = final
    packed_grad = jnp.concatenate(
        [input_acc.astype(jnp.bfloat16), jnp.zeros((1, feature_width), jnp.bfloat16)]
    )
    packed_gate = jnp.concatenate([gate_acc.astype(jnp.bfloat16), jnp.zeros((1,), jnp.bfloat16)])
    back_grad = packed_grad[unpack].reshape(owners, capacity, feature_width)
    back_gate = packed_gate[unpack].reshape(owners, capacity)
    ret_grad, ret_gate = (
        lax.all_to_all(back_grad, "expert", split_axis=0, concat_axis=0, tiled=True),
        lax.all_to_all(back_gate, "expert", split_axis=0, concat_axis=0, tiled=True),
    )
    slot_grad = ret_grad.reshape(recv_slots, feature_width)[target].reshape(
        tok_rows, 2, feature_width
    )
    token_grad = slot_grad.astype(jnp.float32).sum(axis=1).astype(jnp.bfloat16)
    gate_grad = ret_gate.reshape(-1)[target].reshape(tok_rows, 2)
    shares = (
        lax.psum_scatter(
            grad_g.astype(jnp.bfloat16), "replica", scatter_dimension=1, tiled=True
        ).astype(jnp.float32),
        lax.psum_scatter(
            grad_u.astype(jnp.bfloat16), "replica", scatter_dimension=1, tiled=True
        ).astype(jnp.float32),
        lax.psum_scatter(
            grad_d.astype(jnp.bfloat16), "replica", scatter_dimension=1, tiled=True
        ).astype(jnp.float32),
    )
    return (
        token_grad,
        gate_grad,
        shares[0].astype(jnp.bfloat16)[None],
        shares[1].astype(jnp.bfloat16)[None],
        shares[2].astype(jnp.bfloat16)[None],
    )


swap_x = [(0, 2), (1, 3), (2, 0), (3, 1)]
swap_core = [(0, 1), (1, 0), (2, 3), (3, 2)]
swap_part = [(0, 1), (1, 0)]


def slot_kernel(slots, joined, later, cuts, splits, lane_ref, part_ref, *rest):
    count_in = slots * (1 if joined else 2)
    ins, rest = rest[:count_in], rest[count_in:]
    own, near, far, far_near = rest[:3], rest[3], rest[4:10], rest[10:16]
    rest = rest[16 + (4 if later else 0) :]
    kept, far_refs, rest = rest[:4], rest[4 : 4 + len(splits)], rest[4 + len(splits) :]
    backs, rest = rest[: len(cuts)], rest[len(cuts) :]
    held, held_down, rows_in, rows_grad, acts, sems = rest[:6]
    near_ref, hidden_send, hidden_keep, scaled_ref = rest[6:10] if later else kept
    _, features, width = held.shape
    half, eighth = features // 2, features // 8
    height = ins[0].shape[0]
    rows = slots * height
    copies = [[] for _ in range(4)]
    first = pl.multiple_of(part_ref[0] * half, half)
    second = pl.multiple_of(half - part_ref[0] * half, half)
    count = 0
    for share, (group, lines) in enumerate(
        ((own, None), (near, None), (far, (first, second)), (far_near, (first, second)))
    ):
        for kind in range(3):
            target = held_down.at[share] if kind == 2 else held.at[2 * share + kind]
            if share == 0:
                pairs = [(own[kind], target)]
            elif share == 1:
                pairs = [(near.at[kind], target)]
            else:
                pairs = [
                    (group[3 * side + kind], target.at[pl.ds(line, half), :])
                    for side, line in enumerate(lines)
                ]
            for source, place in pairs:
                copies[share].append(pltpu.make_async_copy(source, place, sems.at[count]))
                count += 1
    for group in copies:
        for copy in group:
            copy.start()
    gates = []
    for slot in range(slots):
        lines = slice(slot * height, (slot + 1) * height)
        grad_ref, begin = (ins[slot], features) if joined else (ins[slots + slot], 0)
        rows_in[lines, :] = ins[slot][:, :features]
        rows_grad[lines, :] = grad_ref[:, begin : begin + features]
        lanes = grad_ref[:, begin + features :].astype(jnp.float32)
        gates.append(jnp.sum(lanes * lane_ref[...], axis=1, keepdims=True))
    gate = jnp.concatenate(gates)
    scaled_ref[:rows, :] = (gate * rows_grad[...].astype(jnp.float32)).astype(jnp.bfloat16)
    gate_sum = jnp.zeros(gate.shape, jnp.float32)
    for share in range(4):
        for copy in copies[share]:
            copy.wait()
        pre_gate = jnp.dot(rows_in[...], held[2 * share], preferred_element_type=jnp.float32)
        pre_up = jnp.dot(rows_in[...], held[2 * share + 1], preferred_element_type=jnp.float32)
        back_proj = jnp.dot(rows_grad[...], held_down[share], preferred_element_type=jnp.float32)
        sigmoid_g = jax.nn.sigmoid(pre_gate)
        activated = pre_gate * sigmoid_g
        hidden_act = activated * pre_up
        gate_sum = gate_sum + jnp.sum(back_proj * hidden_act, axis=1, keepdims=True)
        grad_hidden = gate * back_proj
        grad_gate = (
            grad_hidden * pre_up * sigmoid_g * (1.0 + pre_gate * (1.0 - sigmoid_g))
        ).astype(jnp.bfloat16)
        grad_up = (grad_hidden * activated).astype(jnp.bfloat16)
        acts[:, 2 * share * width : (2 * share + 1) * width] = grad_gate
        acts[:, (2 * share + 1) * width : 2 * (share + 1) * width] = grad_up
        hidden = hidden_send if share % 2 else hidden_keep
        pick = share // 2
        hidden[:rows, pick * width : (pick + 1) * width] = hidden_act.astype(jnp.bfloat16)
    near_ref[:rows, :] = acts[:, : 4 * width]
    for far_ref, (begin, end) in zip(far_refs, splits):
        far_ref[...] = acts[begin:end, 4 * width :]
    stores = []
    if later:
        for place, source in enumerate((near_ref, hidden_send, hidden_keep, scaled_ref)):
            target = kept[place].at[pl.ds(kept[place].shape[0] - rows, rows), :]
            stores.append(pltpu.make_async_copy(source, target, sems.at[count + place]))
        for store in stores:
            store.start()
    for piece in range(8):
        lines = slice(piece * eighth, (piece + 1) * eighth)
        part = sum(
            lax.dot_general(
                acts[:, k * width : (k + 1) * width],
                held[k, lines, :],
                (((1,), (1,)), ((), ())),
                preferred_element_type=jnp.float32,
            )
            for k in range(8)
        ).astype(jnp.bfloat16)
        for back, (slot, begin, end) in zip(backs, cuts):
            if begin <= piece * eighth < end:
                back[:, piece * eighth - begin : (piece + 1) * eighth - begin] = part[
                    slot * height : (slot + 1) * height
                ]
    for back, (slot, begin, end) in zip(backs, cuts):
        if end > features:
            back[:, features - begin :] = jnp.broadcast_to(
                gate_sum[slot * height : (slot + 1) * height], (height, 128)
            ).astype(jnp.bfloat16)
    for store in stores:
        store.wait()


def slot_compute(ins, grads, lane, part, weights, total, cuts, splits, kept=()):
    slots = len(ins)
    height = ins[0].shape[0]
    rows = slots * height
    features, width = weights[0].shape
    bf = jnp.bfloat16
    columns = [4 * width, 2 * width, 2 * width, features]
    shapes = [(total, c) for c in columns] + [(end - begin, 4 * width) for begin, end in splits]
    shapes += [(height, end - begin) for _, begin, end in cuts]
    vmem = pl.BlockSpec(memory_space=pltpu.VMEM)
    anywhere = pl.BlockSpec(memory_space=pl.ANY)
    operands = [lane, part, *ins, *grads, *weights, *kept]
    out = pl.pallas_call(
        functools.partial(slot_kernel, slots, not grads, bool(kept), cuts, splits),
        out_shape=[jax.ShapeDtypeStruct(shape, bf) for shape in shapes],
        in_specs=[vmem, pl.BlockSpec(memory_space=pltpu.SMEM)]
        + [vmem] * (len(ins) + len(grads))
        + [anywhere] * (16 + len(kept)),
        out_specs=[anywhere if kept else vmem] * 4 + [vmem] * (len(shapes) - 4),
        scratch_shapes=[
            pltpu.VMEM((8, features, width), bf),
            pltpu.VMEM((4, features, width), bf),
            pltpu.VMEM((rows, features), bf),
            pltpu.VMEM((rows, features), bf),
            pltpu.VMEM((rows, 8 * width), bf),
            pltpu.SemaphoreType.DMA((22,)),
        ]
        + [pltpu.VMEM((rows, c), bf) for c in columns if kept],
        input_output_aliases={len(operands) - len(kept) + i: i for i in range(len(kept))},
        compiler_params=pltpu.CompilerParams(vmem_limit_bytes=48 * 1024 * 1024),
        cost_estimate=pl.CostEstimate(
            flops=rows * features, bytes_accessed=2 * rows * features, transcendentals=0
        ),
    )(*operands)
    return out[:4], out[4 : 4 + len(splits)], out[4 + len(splits) :]


def tied(*values):
    return lax.optimization_barrier(values)


def over_z(value, pairs):
    return lax.ppermute(value, "expert", pairs)


def over_x(value):
    return lax.ppermute(value, "replica", swap_x)


def over_core(value):
    return lax.ppermute(value, "replica", swap_core)


def over_parts(value):
    return lax.ppermute(value, "parts", swap_part)


def apart(step):
    return [(i, i ^ step) for i in range(4)]


def outer(lhs, rhs):
    return lax.dot_general(lhs, rhs, (((0,), (0,)), ((), ())), preferred_element_type=jnp.float32)


def fast_body(tokens, out_grad, expert_ids, gates, gate_weight, up_weight, down_weight):
    z = lax.axis_index("expert")
    y = lax.axis_index("parts")
    rows, features = tokens.shape
    bf, f32 = jnp.bfloat16, jnp.float32
    half = features // 2
    own = [gate_weight[0], up_weight[0], down_weight[0]]
    width = own[0].shape[1]
    halves = [lax.dynamic_slice_in_dim(w, y * half, half, 0) for w in own]
    lanes = jnp.arange(128, dtype=jnp.int32)[None, :]
    gate_lanes = sum(
        jnp.where(expert_ids[:, k : k + 1] == lanes, gates[:, k : k + 1], 0) for k in range(2)
    ).astype(bf)
    lane = (lanes == z).astype(f32)
    wide_grad = jnp.concatenate([out_grad, gate_lanes], axis=1)
    part_index = jnp.reshape(y, (1,)).astype(jnp.int32)

    in_two, in_one = over_z(tokens, apart(2)), over_z(tokens, apart(1))
    across = [over_x(w) for w in halves[:2]]
    other = [over_parts(across[0])]
    in_two, in_one, across[0], across[1], other[0], wide_grad, tokens_x, half_down, stacked = tied(
        in_two, in_one, *across, *other, wide_grad, tokens, halves[2], jnp.stack(own)
    )

    grad_two, grad_one = over_z(wide_grad, apart(2)), over_z(wide_grad, apart(1))
    across.append(over_x(half_down))
    other.append(over_parts(across[1]))
    near = over_core(stacked)
    across[2], near, tokens_x = tied(across[2], near, tokens_x)
    other.append(over_parts(across[2]))
    far_a = over_x(tokens_x)
    in_bc = jnp.concatenate([in_one, in_two])
    two = jnp.concatenate([in_two, grad_two], axis=1)
    two, grad_one, in_bc, far_a, *far_weights = tied(
        two, grad_one, in_bc, far_a, *across, *other
    )

    three = over_z(two, apart(1))
    far_bc = over_x(in_bc)
    weights = [*own, near, *far_weights, *[over_core(w) for w in far_weights]]
    slots, wide, cut = 4, features + 128, features * 3 // 4
    kept, (crossing_abc,), backs = slot_compute(
        [tokens, in_one, in_two],
        [wide_grad, grad_one, grad_two],
        lane,
        part_index,
        weights,
        slots * rows,
        ((0, 0, wide), (1, 0, wide), (2, 0, cut), (2, cut, wide)),
        ((0, 3 * rows),),
    )
    three, far_bc, crossing_abc, *backs = tied(three, far_bc, crossing_abc, *backs)
    back_a, back_b, back_low, back_high = backs

    far_acts_abc = over_x(crossing_abc)
    back_two_low = over_z(back_low, apart(2))
    far_d_low = over_z(far_bc[rows:, :half], apart(1))
    kept, (crossing_d,), (back_d,) = slot_compute(
        [three], [], lane, part_index, weights, slots * rows, ((0, 0, wide),), ((0, rows),), kept
    )
    acts, hidden_send, hidden_keep, scaled = kept
    send = outer(scaled, hidden_send).astype(bf)
    far_acts_abc, back_two_low, far_d_low, crossing_d, back_d, back_high, acts, send, scaled = tied(
        far_acts_abc, back_two_low, far_d_low, crossing_d, back_d, back_high, acts, send, scaled
    )

    far_acts_d = over_x(crossing_d)
    back_two_high = over_z(back_high, apart(2))
    far_d_high = over_z(far_bc[rows:, half:], apart(1))
    keep = outer(scaled, hidden_keep).astype(bf)
    both = keep.astype(f32) + over_core(send).astype(f32)
    crossing, both = both[:, width:].astype(bf), both[:, :width].astype(bf)
    rows_first = jnp.concatenate([tokens, in_bc, three[:, :features], far_a, far_bc[:rows]])
    acts_first = jnp.concatenate([acts, far_acts_abc[: 2 * rows]])
    first_keep = outer(rows_first, acts_first[:, : 2 * width]).astype(bf)
    far_acts_d, back_two_high, far_d_high, crossing, both, back_d, back_b, first_keep = tied(
        far_acts_d, back_two_high, far_d_high, crossing, both, back_d, back_b, first_keep
    )
    first_send = outer(rows_first, acts_first[:, 2 * width :]).astype(bf)

    down_far = over_x(crossing)
    back_three = over_z(back_d, apart(3))
    back_one = over_z(back_b, apart(1))
    back_two = jnp.concatenate([back_two_low, back_two_high], axis=1)
    rows_last = jnp.concatenate(
        [far_bc[rows:], jnp.concatenate([far_d_low, far_d_high], axis=1)]
    )
    acts_last = jnp.concatenate([far_acts_abc[2 * rows :], far_acts_d])
    send, keep = (
        outer(rows_last, acts_last[:, cols]) + first.astype(f32)
        for cols, first in (
            (slice(2 * width, None), first_send),
            (slice(0, 2 * width), first_keep),
        )
    )
    send = send.astype(bf)
    got = over_core(send)
    pair = (keep + got.astype(f32)).astype(bf)
    gate_out, up_out = pair[:, :width], pair[:, width:]
    back_one, back_three, down_far, gate_out, up_out = tied(
        back_one, back_three, down_far, gate_out, up_out
    )
    returned = [back_a, back_one, back_two, back_three]
    down = (both.astype(f32) + down_far.astype(f32)).astype(bf)
    token_grad = sum(r[:, :features].astype(f32) for r in returned).astype(bf)
    gate_grad = sum(
        jnp.where(expert_ids == (z ^ step), r[:, features : features + 1].astype(f32), 0.0)
        for step, r in enumerate(returned)
    ).astype(bf)
    return token_grad, gate_grad, gate_out[None], up_out[None], down[None]


def body(*args):
    sizes = tuple(lax.axis_size(name) for name in ("parts", "expert", "replica"))
    if sizes == (2, 4, 4):
        return fast_body(*args)
    return general_body(*args)


def solution(mesh):
    in_specs = (
        P(("parts", "expert", "replica"), None),
        P(("parts", "expert", "replica"), None),
        P(("parts", "expert", "replica"), None),
        P(("parts", "expert", "replica"), None),
        P("expert", None, "replica"),
        P("expert", None, "replica"),
        P("expert", None, "replica"),
    )
    out_specs = (
        P(("parts", "expert", "replica"), None),
        P(("parts", "expert", "replica"), None),
        P(("parts", "expert"), None, "replica"),
        P(("parts", "expert"), None, "replica"),
        P(("parts", "expert"), None, "replica"),
    )
    return jax.shard_map(body, mesh=mesh, in_specs=in_specs, out_specs=out_specs, check_vma=False)
```
